32 devices in a mesh: section: 4 (over y, x), dp: 8 (over z, core).
Axes of the slice: x: 2, y: 2, z: 4, core: 2. Of those that a mesh axis runs over, the one named last changes fastest.
Arguments:
- layer_input: bfloat16 [16, 1024, 512], P('dp'), may hold values from -6 to 6
- resets: int32 [16, 1024], P('dp'), may hold values 0 or 1
- first_weights: bfloat16 [4, 512, 2048], P('section'), may hold values from -0.25 to 0.25
- second_weights: bfloat16 [4, 2048, 512], P('section'), may hold values from -1.5 to 1.5
- section_vectors: float32 [4, 3584], P('section'), may hold values from -8 to 2, as said below
- cotangent: bfloat16 [16, 1024, 512], P('dp'), may hold values from -6 to 6
Outputs:
- section_outputs: bfloat16 [4, 16, 1024, 512], P('section', 'dp')
- section_grads: bfloat16 [4, 16, 1024, 512], P('section', 'dp')
- first_grads: float32 [4, 512, 2048], P('section', 'dp')
- second_grads: float32 [4, 2048, 512], P('section', 'dp')
- vector_grads: float32 [4, 3584], P('section', 'dp')
The draws below stay inside these ranges and needn't reach their ends.
Inputs may be any that keep to these rules, and one draw needn't show every extreme that they name: `resets`: 1 marks a token that starts a new document inside its row. `section_vectors`: row k holds sub-layer k's norm gain in its first 512 entries, then for a mixer 4 blocks of 512 convolution taps and 1024 update biases, for a feed-forward 2048 hidden biases, 512 output scales and 512 output biases.
All inputs are finite; a program needn't handle non-finite values. No bound on the sum of `resets` on one device may be relied on, other than what follows from the above.
Results may differ from the reference program's by a relative error of at most 0.018.
Values may be sent and summed in bfloat16 or wider, within the bound.
No kernel may reach another device: no remote copies, remote signals or barrier semaphores. Data moves between devices by JAX's collectives and lax.ppermute only.
A program may use at most 320 MiB of HBM per device.

```python
import jax
import jax.numpy as jnp
from jax import lax

D = 512
H = 1024
FF = 2048
KCONV = 4
SUBLAYERS = 4
L = 1024
MICRO = 2
ROWS = 16
N_DP = 8


def draw_section_vectors(key, part):
    gain_key, rest_key, bias_key, scale_key, shift_key = jax.random.split(jax.random.fold_in(key, 11), 5)
    gains = jax.random.uniform(gain_key, (SUBLAYERS, D), jnp.float32, 0.7, 1.3)
    rests = jnp.clip(0.5 * jax.random.normal(rest_key, (SUBLAYERS, FF), jnp.float32), -2.0, 2.0)
    update_bias = jax.random.uniform(bias_key, (SUBLAYERS, H), jnp.float32, -7.0, -2.5)
    out_scale = jax.random.uniform(scale_key, (SUBLAYERS, D), jnp.float32, 0.7, 1.3)
    out_bias = jnp.clip(0.2 * jax.random.normal(shift_key, (SUBLAYERS, D), jnp.float32), -0.8, 0.8)
    layer_parity = (jnp.arange(SUBLAYERS) % 2)[:, None]
    tail = jnp.where(layer_parity == 0, update_bias, jnp.concatenate([out_scale, out_bias], axis=1))
    return jnp.concatenate([gains, rests, tail], axis=1)


def draw_second_weights(key, part):
    base = jnp.clip(jax.random.normal(jax.random.fold_in(key, 23), (SUBLAYERS, FF, D), jnp.float32), -6.0, 6.0)
    layer_index = jnp.arange(SUBLAYERS)[:, None, None]
    row_index = jnp.arange(FF)[None, :, None]
    mixer_scale = jnp.where(row_index < H, 8.0 * H ** (-0.5), 2.0 * D ** (-0.5))
    scale = jnp.where(layer_index % 2 == 0, mixer_scale, H ** (-0.5))
    return (base * scale).astype(jnp.bfloat16)


def plant(drawn, stream_key, smallest, high):
    index_at = [jax.random.randint(jax.random.fold_in(stream_key, axis), (), 0, length) for axis, length in enumerate(drawn.shape)]
    main_axis = drawn.shape.index(max(drawn.shape))
    neighbour = index_at[:main_axis] + [(index_at[main_axis] + 1) % drawn.shape[main_axis]] + index_at[main_axis + 1:]
    return drawn.at[tuple(index_at)].set(smallest).at[tuple(neighbour)].set(high)


def level_of(rng, dims, shards, low, top_value):
    factor_of, own = 1.0, jax.random.fold_in(rng, 6)
    for dim, blocks in shards:
        heights = jnp.exp(jax.random.uniform(jax.random.fold_in(own, dim), (blocks,), jnp.float32, low / len(shards), top_value / len(shards)))
        factor_of = factor_of * jnp.repeat(heights, dims[dim] // blocks).reshape([-1 if axis == dim else 1 for axis in range(len(dims))])
    return factor_of


def gaussian(rng, dims, spread, limit, shards=(), dtype=jnp.bfloat16):
    array = jax.random.normal(rng, dims, jnp.float32) * spread
    if len(shards) > 0:
        array = level_of(rng, dims, shards, -0.22, 0.18) * array
    return jnp.clip(array, min=-limit, max=limit).astype(dtype)


def setup_inputs(seed: int = 0) -> dict:
    key_of = jax.random.split(jax.random.key(seed), 7)
    return {
        "layer_input": gaussian(key_of[0], (ROWS, L, D), 1.0, 6.0, ((0, 8),)),
        "resets": plant((jax.random.randint(key_of[1], (ROWS, L), 0, 256) < 1).astype(jnp.int32), jax.random.fold_in(key_of[1], 1), 0, 1),
        "first_weights": gaussian(key_of[2], (SUBLAYERS, D, FF), D ** -0.5, 0.25, ((0, 4),)),
        "second_weights": draw_second_weights(jax.random.fold_in(key_of[6], 71), 0),
        "section_vectors": draw_section_vectors(jax.random.fold_in(key_of[6], 71), 0),
        "cotangent": gaussian(key_of[5], (ROWS, L, D), 1.0, 6.0, ((0, 8),)),
    }


@jax.custom_vjp
def low(v):
    return lax.optimization_barrier(v.astype(jnp.bfloat16)).astype(jnp.float32)

@jax.custom_vjp
def low_back(v):
    return v

def low_keep(v):
    return (low(v), None)

def low_pass(kept, grad):
    return (grad,)

def back_keep(v):
    return (v, None)

def back_low(kept, grad):
    return (low(grad),)
low.defvjp(low_keep, low_pass)
low_back.defvjp(back_keep, back_low)
norm_eps = 1e-05

def norm_piece(values, norm_gain):
    factor = lax.rsqrt(lax.optimization_barrier(jnp.mean(values * values, axis=-1, keepdims=True)) + norm_eps)
    return values * factor * norm_gain

def causal_conv(normed, conv_taps, document_ids):
    summed = normed * conv_taps[0]
    for offset in range(1, KCONV):
        shifted = jnp.pad(normed, ((0, 0), (offset, 0), (0, 0)))[:, :-offset]
        earlier = jnp.pad(document_ids, ((0, 0), (offset, 0)), constant_values=-1)[:, :-offset]
        summed = summed + jnp.where((earlier == document_ids)[..., None], shifted, 0.0) * conv_taps[offset]
    return summed

def linear_step(earlier, later):
    return (earlier[0] * later[0], later[0] * earlier[1] + later[1])

def mixer_layer(values, norm_gain, conv_taps, update_bias, w_in, w_gate, w_out, keep_mask, document_ids):
    normed = norm_piece(values, norm_gain)
    conv = causal_conv(normed, conv_taps, document_ids)
    bias_row = jnp.concatenate([update_bias, jnp.zeros((H,), jnp.float32)])
    projected = low_back(jnp.einsum('rtd,df->rtf', low(conv), w_in, precision=lax.Precision.HIGHEST) + bias_row)
    gate_pre = low_back(jnp.einsum('rtd,hd->rth', low(normed), w_gate, precision=lax.Precision.HIGHEST))
    update = jax.nn.sigmoid(projected[..., :H])
    decays = (1.0 - update) * keep_mask[..., None]
    states = lax.associative_scan(linear_step, (decays, update * projected[..., H:]), axis=1)[1]
    merged = low(states * jax.nn.silu(gate_pre))
    return jnp.einsum('rth,hd->rtd', merged, w_out, precision=lax.Precision.HIGHEST)

def feed_forward(values, norm_gain, hidden_bias, out_scale, out_bias, w_up, w_down):
    normed = low(norm_piece(values, norm_gain))
    hidden_pre = low_back(jnp.einsum('rtd,df->rtf', normed, w_up, precision=lax.Precision.HIGHEST) + hidden_bias)
    active = low(jax.nn.gelu(hidden_pre))
    down = low_back(jnp.einsum('rtf,fd->rtd', active, w_down, precision=lax.Precision.HIGHEST))
    return down * out_scale + out_bias

def network(first_all, second_all, vectors, values, boundary_zeros, keep_mask, document_ids):
    stream = low_back(values)
    outputs = []
    for sublayer in range(SUBLAYERS):
        norm_gain = vectors[sublayer, :D]
        vector_rest = vectors[sublayer, D:]
        if sublayer % 2 == 0:
            branch = mixer_layer(stream, norm_gain, vector_rest[:FF].reshape(KCONV, D), vector_rest[FF:], first_all[sublayer], second_all[sublayer, H:], second_all[sublayer, :H], keep_mask, document_ids)
        else:
            branch = feed_forward(stream, norm_gain, vector_rest[:FF], vector_rest[FF:FF + D], vector_rest[FF + D:], first_all[sublayer], second_all[sublayer])
        summed = stream + branch
        if sublayer + 1 < SUBLAYERS:
            stream = low_back(low(summed + boundary_zeros[sublayer]))
        else:
            stream = low(summed)
        outputs.append(stream)
    return jnp.stack(outputs)

def reference(layer_input, resets, first_weights, second_weights, section_vectors, cotangent):
    first_all = first_weights.astype(jnp.float32)
    second_all = second_weights.astype(jnp.float32)
    vectors = section_vectors.astype(jnp.float32)
    group_inputs = layer_input.reshape(N_DP, MICRO, L, D)
    group_resets = resets.reshape(N_DP, MICRO, L)
    group_cots = cotangent.reshape(N_DP, MICRO, L, D)

    def group_step(grad_totals, group_item):
        inputs_now, resets_now, cots_now = group_item
        keep_mask = 1.0 - resets_now.astype(jnp.float32)
        document_ids = jnp.cumsum(resets_now, axis=1).astype(jnp.int32)
        boundary_zeros = jnp.zeros((SUBLAYERS - 1, MICRO, L, D), jnp.float32)

        def forward_pass(first_now, second_now, vectors_now, values, zeros_now):
            return network(first_now, second_now, vectors_now, values, zeros_now, keep_mask, document_ids)
        outputs, pullback = jax.vjp(forward_pass, first_all, second_all, vectors, inputs_now.astype(jnp.float32), boundary_zeros)
        output_grads = jnp.concatenate([jnp.zeros((SUBLAYERS - 1, MICRO, L, D), jnp.float32), cots_now.astype(jnp.float32)[None]], axis=0)
        grad_first, grad_second, grad_vectors, grad_values, grad_bounds = pullback(output_grads)
        backward_rows = jnp.concatenate([grad_values[None], grad_bounds], axis=0)
        grad_totals = (grad_totals[0] + grad_first, grad_totals[1] + grad_second, grad_totals[2] + grad_vectors)
        return (grad_totals, (outputs.astype(jnp.bfloat16), backward_rows.astype(jnp.bfloat16)))
    start_totals = (jnp.zeros((SUBLAYERS, D, FF), jnp.float32), jnp.zeros((SUBLAYERS, FF, D), jnp.float32), jnp.zeros((SUBLAYERS, D + FF + H), jnp.float32))
    grad_totals, (outputs, backward_rows) = lax.scan(group_step, start_totals, (group_inputs, group_resets, group_cots))
    section_outputs = jnp.transpose(outputs, (1, 0, 2, 3, 4)).reshape(SUBLAYERS, ROWS, L, D)
    section_grads = jnp.transpose(backward_rows, (1, 0, 2, 3, 4)).reshape(SUBLAYERS, ROWS, L, D)
    grad_scale = (ROWS * L) ** (-0.5)
    return (section_outputs, section_grads, grad_totals[0] * grad_scale, grad_totals[1] * grad_scale, grad_totals[2] * grad_scale)
```

```python
import functools
import typing

import jax
import jax.numpy as jnp
from jax import lax
from jax.experimental import pallas as pl
from jax.experimental.pallas import tpu as pltpu
from jax.sharding import PartitionSpec as P

norm_eps = 1e-05
chunk_rows = 128
hop_ticks = 3
lane_block = 256
vmem_mib = 8
f32 = jnp.float32
bf16 = jnp.bfloat16
VMEM = pltpu.VMEM


def resident(array):
    return pltpu.with_memory_space_constraint(array, VMEM)


def nn(left, right):
    return jnp.dot(left, right, preferred_element_type=f32)


def nt(left, right):
    return lax.dot_general(left, right, (((1,), (1,)), ((), ())), preferred_element_type=f32)


def tn(left, right):
    return lax.dot_general(left, right, (((0,), (0,)), ((), ())), preferred_element_type=f32)


def logistic(v):
    return 1.0 / (1.0 + jnp.exp(-v))


def by_eight(v):
    return jnp.sum(v.reshape(v.shape[0] // 8, 8, v.shape[1]), axis=0)


def spread(ref, value):
    for k in range(ref.shape[0]):
        ref[k] = value[:, 128 * k : 128 * (k + 1)]


def gathered(ref):
    return jnp.concatenate([ref[k] for k in range(ref.shape[0])], axis=1)


def scan_segments(a_ref, b_ref, carry, backward):
    tiles, total, lanes = b_ref.shape
    steps = total // 8
    order = range(steps - 1, -1, -1) if backward else range(steps)
    run, prod = [None] * tiles, [None] * tiles
    for i in order:
        rows = pl.ds(i, 8, stride=steps)
        for k in range(tiles):
            a = a_ref[k, rows, :]
            b = b_ref[k, rows, :]
            if run[k] is None:
                run[k], prod[k] = (a * b if backward else b), a
            elif backward:
                b = b + run[k]
                b_ref[k, rows, :] = b
                a_ref[k, rows, :] = prod[k]
                run[k], prod[k] = a * b, prod[k] * a
            else:
                run[k] = a * run[k] + b
                prod[k] = prod[k] * a
                b_ref[k, rows, :] = run[k]
                a_ref[k, rows, :] = prod[k]
    place = lax.broadcasted_iota(jnp.int32, (8, lanes), 0)
    inward, last = [], []
    for k in range(tiles):
        held = carry[:, lanes * k : lanes * (k + 1)]
        r, p = run[k], prod[k]
        for d in (1, 2, 4):
            seen = place < 8 - d if backward else place >= d
            shift = 8 - d if backward else d
            p_before = jnp.where(seen, pltpu.roll(p, shift, 0), 1.0)
            r_before = jnp.where(seen, pltpu.roll(r, shift, 0), 0.0)
            r = r + p * r_before
            p = p * p_before
        ends = r + p * held
        if backward:
            inward.append(jnp.where(place < 7, pltpu.roll(ends, 7, 0), held))
            last.append(ends[0:1, :])
        else:
            inward.append(jnp.where(place >= 1, pltpu.roll(ends, 1, 0), held))
            last.append(ends[7:8, :])
    for i in order:
        rows = pl.ds(i, 8, stride=steps)
        for k in range(tiles):
            if backward and i == steps - 1:
                b_ref[k, rows, :] = b_ref[k, rows, :] + inward[k]
            else:
                b_ref[k, rows, :] = b_ref[k, rows, :] + a_ref[k, rows, :] * inward[k]
    return jnp.concatenate(last, axis=1)


def norm_factor(x):
    return lax.rsqrt(jnp.mean(x * x, axis=-1, keepdims=True) + norm_eps)


def parts_of(held, width, ff):
    cuts = [width * i for i in range(7)] + [6 * width + ff, 6 * width + 2 * ff]
    return [held.at[:, lo:hi] for lo, hi in zip(cuts, cuts[1:])]


class Plan(typing.NamedTuple):
    hop: int
    chunks: int
    per_row: int
    sections: int


def forward_turn(plan, info):
    c = info[2] - plan.hop * info[0]
    return jnp.clip(c, 0, plan.chunks - 1), (c >= 0) & (c < plan.chunks)


def backward_turn(plan, info):
    j = info[3] - plan.hop * (plan.sections - 1 - info[0])
    return jnp.clip(j, 0, plan.chunks - 1), (j >= 0) & (j < plan.chunks)


def backward_chunk(plan, j):
    behind = lax.rem(j, plan.per_row)
    return j - behind + plan.per_row - 1 - behind


def forward_kernel(
    plan, recv, w1, w2, vec, msk,
    sc_in, held_in, hs_in, nh_in, send, sc, held, hs, nh,
    a_s, b_s, g_s, nx, mg,
):
    rows_now, width = recv.shape
    ff = w1.shape[1]
    xs, nb, cv, _, outs, _, wide_a, wide_b = parts_of(held, width, ff)
    hidden = ff // 2
    c, active = forward_turn(plan, sc)
    start = pl.multiple_of(c * rows_now, rows_now)
    rows = pl.ds(start, rows_now)
    mixer = sc[1] == 0
    gain = vec[:, :width]
    tail = width + ff

    @pl.when(active & (sc[0] > 0))
    def _():
        xs[rows, :] = recv[...]

    @pl.when(active & mixer)
    def _():
        x = xs[rows, :].astype(f32)
        normed = x * norm_factor(x) * gain
        nx[0:8, :] = nh[...]
        nx[8:, :] = normed
        nh[...] = nx[rows_now:, :]
        conv = normed * vec[:, width : 2 * width]
        taps = ff // width
        for j in range(1, taps):
            tap = vec[:, (1 + j) * width : (2 + j) * width]
            conv = conv + nx[8 - j : 8 - j + rows_now, :] * msk[rows, j - 1 : j] * tap
        conv16 = conv.astype(bf16)
        norm16 = normed.astype(bf16)
        cv[rows, :] = conv16
        nb[rows, :] = norm16
        keep = msk[rows, 0:1]
        for lo in range(0, hidden, lane_block):
            hi = lo + lane_block
            update = logistic(nn(conv16, w1[:, lo:hi]) + vec[:, tail + lo : tail + hi])
            candidate = nn(conv16, w1[:, hidden + lo : hidden + hi])
            g_s[...] = nt(norm16, w2[hidden + lo : hidden + hi, :])
            wide_a[rows, lo:hi] = update.astype(bf16)
            wide_a[rows, hidden + lo : hidden + hi] = candidate.astype(bf16)
            spread(a_s, (1.0 - update) * keep)
            spread(b_s, update * candidate)
            hs[0:1, lo:hi] = scan_segments(a_s, b_s, hs[0:1, lo:hi], False)
            states = gathered(b_s)
            gate = g_s[...]
            wide_b[rows, lo:hi] = states.astype(bf16)
            wide_b[rows, hidden + lo : hidden + hi] = gate.astype(bf16)
            mg[:, lo:hi] = (states * gate * logistic(gate)).astype(bf16)
        result = (x + nn(mg[...], w2[:hidden, :])).astype(bf16)
        send[...] = result
        outs[rows, :] = result

    @pl.when(active & jnp.logical_not(mixer))
    def _():
        x = xs[rows, :].astype(f32)
        norm16 = (x * norm_factor(x) * gain).astype(bf16)
        cv[rows, :] = norm16
        for lo in range(0, ff, lane_block):
            hi = lo + lane_block
            h = nn(norm16, w1[:, lo:hi]) + vec[:, width + lo : width + hi]
            wide_a[rows, lo:hi] = h.astype(bf16)
            inner = 0.7978845608 * (h + 0.044715 * (h * h * h))
            wide_b[rows, lo:hi] = (0.5 * h * (1.0 + jnp.tanh(inner))).astype(bf16)
        down = nn(wide_b[rows, :], w2[...])
        nb[rows, :] = down.astype(bf16)
        branch = down * vec[:, tail : tail + width] + vec[:, tail + width : tail + 2 * width]
        result = (x + branch).astype(bf16)
        send[...] = result
        outs[rows, :] = result

    sc[2] = sc[2] + 1


def norm_backward(x, factor, gain, grad_normed, grads_wide, vacc):
    width = x.shape[1]
    scaled = x * factor
    vacc[:, :width] = vacc[:, :width] + by_eight(grad_normed * scaled)
    e = grad_normed * gain
    level = jnp.mean(e * scaled, axis=-1, keepdims=True)
    return (grads_wide + factor * (e - scaled * level)).astype(bf16)


def backward_kernel(
    plan, recv, w1, w2, vec, msk,
    sc_in, held_in, vacc_in, wc_in, gh_in, send, sc, held, vacc, wc, gh,
    a_s, b_s, st, nx, gx,
):
    rows_now, width = recv.shape
    ff = w1.shape[1]
    xs, nb, _, gs, _, grads, wide_a, wide_b = parts_of(held, width, ff)
    hidden = ff // 2
    j, active = backward_turn(plan, sc)
    start = pl.multiple_of(backward_chunk(plan, j) * rows_now, rows_now)
    rows = pl.ds(start, rows_now)
    before = pl.ds(pl.multiple_of(jnp.maximum(start - 16, 0), 16), 16)
    mixer = sc[1] == 0
    gain = vec[:, :width]
    tail = width + ff

    @pl.when(active & (sc[0] < plan.sections - 1))
    def _():
        gs[rows, :] = recv[...]

    @pl.when(active & mixer)
    def _():
        g16 = gs[rows, :]
        keep = msk[rows, 0:1]
        grad_normed = jnp.zeros((rows_now, width), f32)
        grad_conv = jnp.zeros((rows_now, width), f32)
        for lo in range(0, hidden, lane_block):
            hi = lo + lane_block
            grad_merged = nt(g16, w2[lo:hi, :])
            gate = wide_b[rows, hidden + lo : hidden + hi].astype(f32)
            st[0:8, :] = wide_b[before, lo:hi].astype(f32)[8:16, :]
            states = wide_b[rows, lo:hi].astype(f32)
            st[8:, :] = states
            sig = logistic(gate)
            act = gate * sig
            wide_b[rows, lo:hi] = (states * act).astype(bf16)
            slope = sig * (1.0 + gate * (1.0 - sig))
            grad_gate = (grad_merged * states * slope).astype(bf16)
            wide_b[rows, hidden + lo : hidden + hi] = grad_gate
            update = wide_a[rows, lo:hi].astype(f32)
            spread(a_s, (1.0 - update) * keep)
            spread(b_s, grad_merged * act)
            wc[0:1, lo:hi] = scan_segments(a_s, b_s, wc[0:1, lo:hi], True)
            candidate = wide_a[rows, hidden + lo : hidden + hi].astype(f32)
            through = gathered(b_s) * update
            grad_up = through * (1.0 - update) * (candidate - keep * st[7 : 7 + rows_now, :])
            up16 = grad_up.astype(bf16)
            cand16 = through.astype(bf16)
            wide_a[rows, lo:hi] = up16
            wide_a[rows, hidden + lo : hidden + hi] = cand16
            at = tail + lo
            vacc[:, at : at + lane_block] = vacc[:, at : at + lane_block] + by_eight(up16.astype(f32))
            grad_normed = grad_normed + nn(grad_gate, w2[hidden + lo : hidden + hi, :])
            grad_conv = grad_conv + nt(up16, w1[:, lo:hi]) + nt(cand16, w1[:, hidden + lo : hidden + hi])
        x = xs[rows, :].astype(f32)
        x_before = xs[before, :].astype(f32)[8:16, :]
        factor = norm_factor(x)
        nx[0:8, :] = x_before * norm_factor(x_before) * gain
        nx[8:, :] = x * factor * gain
        gx[0:rows_now, :] = grad_conv
        gx[rows_now:, :] = gh[...]
        gh[...] = gx[0:8, :]
        taps = ff // width
        for j in range(taps):
            at = (1 + j) * width
            tap = vec[:, at : at + width]
            if j == 0:
                grad_normed = grad_normed + tap * grad_conv
                piece = grad_conv * nx[8:, :]
            else:
                ahead = gx[j : j + rows_now, :] * msk[rows, 2 + j : 3 + j]
                grad_normed = grad_normed + tap * ahead
                piece = grad_conv * (nx[8 - j : 8 - j + rows_now, :] * msk[rows, j - 1 : j])
            vacc[:, at : at + width] = vacc[:, at : at + width] + by_eight(piece)
        result = norm_backward(x, factor, gain, grad_normed, g16.astype(f32), vacc)
        send[...] = result
        grads[rows, :] = result

    @pl.when(active & jnp.logical_not(mixer))
    def _():
        grads_wide = gs[rows, :].astype(f32)
        down16 = (grads_wide * vec[:, tail : tail + width]).astype(bf16)
        down = nb[rows, :].astype(f32)
        at = tail
        vacc[:, at : at + width] = vacc[:, at : at + width] + by_eight(grads_wide * down)
        at = tail + width
        vacc[:, at : at + width] = vacc[:, at : at + width] + by_eight(grads_wide)
        gs[rows, :] = down16
        nb[rows, :] = down16
        for lo in range(0, ff, lane_block):
            hi = lo + lane_block
            grad_active = nt(down16, w2[lo:hi, :])
            h = wide_a[rows, lo:hi].astype(f32)
            square = h * h
            inner = 0.7978845608 * h * (1.0 + 0.044715 * square)
            bend = jnp.tanh(inner)
            slope = 0.5 * (1.0 + bend) + (0.5 * 0.7978845608) * h * (1.0 - bend * bend) * (
                1.0 + (3.0 * 0.044715) * square
            )
            hid16 = (grad_active * slope).astype(bf16)
            wide_a[rows, lo:hi] = hid16
            at = width + lo
            vacc[:, at : at + lane_block] = vacc[:, at : at + lane_block] + by_eight(hid16.astype(f32))
        grad_normed = nt(wide_a[rows, :], w1[...])
        x = xs[rows, :].astype(f32)
        factor = norm_factor(x)
        result = norm_backward(x, factor, gain, grad_normed, grads_wide, vacc)
        send[...] = result
        grads[rows, :] = result


def weight_kernel(
    plan, unit, sc_in, held_in, dw1_in, dw2_in, sc, held, dw1, dw2,
):
    width, ff = dw1.shape
    hidden = ff // 2
    _, nb, cv, gs, _, _, wide_a, wide_b = parts_of(held, width, ff)
    j, active = backward_turn(plan, sc)
    due = active & (lax.rem(j, unit) == unit - 1)
    size = unit * chunk_rows
    at = backward_chunk(plan, j) // unit
    rows = pl.ds(pl.multiple_of(at * size, size), size)
    step = 2 * lane_block

    def add(fresh):
        conv = cv[rows, :]
        for lo in range(0, ff, step):
            term = tn(conv, wide_a[rows, lo : lo + step])
            dw1[:, lo : lo + step] = term if fresh else dw1[:, lo : lo + step] + term
        for half, side in enumerate((gs, nb)):
            left = side[rows, :]
            for lo in range(half * hidden, (half + 1) * hidden, step):
                term = tn(left, wide_b[rows, lo : lo + step])
                dw2[:, lo : lo + step] = term if fresh else dw2[:, lo : lo + step] + term

    @pl.when(due & (j < unit))
    def _():
        add(True)

    @pl.when(due & (j >= unit))
    def _():
        add(False)

    sc[3] = sc[3] + 1


def load_kernel(place, x_hbm, g_hbm, w1_hbm, w2_hbm, vec_hbm, msk_hbm,
                info, held, w1, w2, vec, msk, hs, nh, wc, gh, vacc, dw1, dw2, blank, sems):
    xs, _, _, gs, _, _, _, _ = parts_of(held, w1.shape[0], w1.shape[1])
    section, sections = place[0], place[1]
    info[0] = section
    info[1] = lax.rem(section, 2)
    info[2] = 0
    info[3] = 0
    moves = [(w1_hbm, w1), (w2_hbm, w2), (vec_hbm, vec), (msk_hbm, msk)]
    copies = [pltpu.make_async_copy(a, b, sems.at[i]) for i, (a, b) in enumerate(moves)]
    first = pltpu.make_async_copy(x_hbm, xs, sems.at[4])
    last = pltpu.make_async_copy(g_hbm, gs, sems.at[5])
    for copy in copies:
        copy.start()

    @pl.when(section == 0)
    def _():
        first.start()

    @pl.when(section == sections - 1)
    def _():
        last.start()

    for ref in (hs, nh, wc, gh, vacc, blank):
        ref[...] = jnp.zeros_like(ref)
    for copy in copies:
        copy.wait()

    @pl.when(section == 0)
    def _():
        first.wait()

    @pl.when(section == sections - 1)
    def _():
        last.wait()


def finish_kernel(held, dw1, dw2, vacc, outs_out, grads_out, first, second, vectors, sems):
    _, _, _, _, outs, grads, _, _ = parts_of(held, dw1.shape[0], dw1.shape[1])
    copies = [pltpu.make_async_copy(outs, outs_out, sems.at[0]), pltpu.make_async_copy(grads, grads_out, sems.at[1])]
    for copy in copies:
        copy.start()
    first[...] = dw1[...].astype(bf16)
    second[...] = dw2[...].astype(bf16)
    vectors[...] = jnp.sum(vacc[...], axis=0, keepdims=True)
    for copy in copies:
        copy.wait()


def forward_scratch(rows, width, hidden):
    return (
        [VMEM((lane_block // 128, rows, 128), f32)] * 2
        + [VMEM((rows, lane_block), f32)]
        + [VMEM((rows + 8, width), f32), VMEM((rows, hidden), bf16)]
    )


def backward_scratch(rows, width):
    return (
        [VMEM((lane_block // 128, rows, 128), f32)] * 2
        + [VMEM((rows + 8, lane_block), f32)]
        + [VMEM((rows + 8, width), f32)] * 2
    )


def params(mib):
    return pltpu.CompilerParams(vmem_limit_bytes=mib * 2**20)


def call(kernel, plain_out, inputs, info, state, scratch, flops, name):
    kept = (pltpu.SMEM(info.shape, info.dtype),) + tuple(VMEM(s.shape, s.dtype) for s in state)
    kept_specs = [pl.BlockSpec(memory_space=pltpu.SMEM)] + [pl.BlockSpec(memory_space=VMEM) for _ in state]
    return pl.pallas_call(
        kernel,
        out_shape=tuple(plain_out) + kept,
        in_specs=[pl.BlockSpec(memory_space=VMEM) for _ in inputs] + kept_specs,
        out_specs=tuple([pl.BlockSpec(memory_space=VMEM) for _ in plain_out] + kept_specs),
        input_output_aliases={len(inputs) + i: len(plain_out) + i for i in range(len(kept))},
        scratch_shapes=scratch,
        compiler_params=params(vmem_mib),
        cost_estimate=pl.CostEstimate(flops=flops, bytes_accessed=0, transcendentals=0),
        name=name,
    )(*inputs, info, *state)


def body(layer_input, resets, first_weights, second_weights, section_vectors, cotangent):
    row_count, seq_length, width = layer_input.shape
    ff = first_weights.shape[2]
    hidden = ff // 2
    vector_width = section_vectors.shape[1]
    section = lax.axis_index("section")
    sections = lax.axis_size("section")
    dp_count = lax.axis_size("dp")
    tokens = row_count * seq_length
    per_row = seq_length // chunk_rows
    chunks = row_count * per_row
    unit_chunks = 2

    keep = 1.0 - resets.astype(f32)
    keep = jnp.concatenate([jnp.zeros((row_count, 1), f32), keep[:, 1:]], axis=1).reshape(-1)

    def later(v, j):
        return jnp.concatenate([jnp.zeros((j,), f32), v[:-j]])

    def sooner(v, j):
        return jnp.concatenate([v[j:], jnp.zeros((j,), f32)])

    m1 = keep
    m2 = keep * later(keep, 1)
    m3 = m2 * later(keep, 2)
    msk = jnp.stack([m1, m2, m3, sooner(m1, 1), sooner(m2, 2), sooner(m3, 3), m1, m1], axis=1)


    made = (
        pltpu.SMEM((4,), jnp.int32), VMEM((tokens, 6 * width + 2 * ff), bf16),
        VMEM((width, ff), bf16), VMEM((ff, width), bf16), VMEM((1, vector_width), f32), VMEM(msk.shape, f32),
        VMEM((8, hidden), f32), VMEM((8, width), f32), VMEM((8, hidden), f32), VMEM((8, width), f32),
        VMEM((8, vector_width), f32), VMEM((width, ff), f32), VMEM((width, ff), f32),
        VMEM((chunk_rows, width), bf16),
    )
    inputs = [
        layer_input.reshape(tokens, width), cotangent.reshape(tokens, width),
        first_weights[0], second_weights[0], section_vectors, msk,
    ]
    info, held, w1, w2, vec, msk, hs, nh, wc, gh, vacc, dw1, dw2, blank = pl.pallas_call(
        load_kernel,
        out_shape=made,
        in_specs=[pl.BlockSpec(memory_space=pltpu.SMEM)] + [pl.BlockSpec(memory_space=pltpu.HBM)] * 6,
        out_specs=(pl.BlockSpec(memory_space=pltpu.SMEM),) + tuple(pl.BlockSpec(memory_space=VMEM) for _ in made[1:]),
        scratch_shapes=[pltpu.SemaphoreType.DMA((6,))],
        compiler_params=params(vmem_mib),
        name="load",
    )(
        jnp.stack([section.astype(jnp.int32), jnp.int32(sections)]),
        *(pltpu.with_memory_space_constraint(v, pltpu.HBM) for v in inputs),
    )
    w1, w2, vec, msk = (resident(v) for v in (w1, w2, vec, msk))

    hop = hop_ticks
    base = per_row - 1 + hop * (sections - 1)
    ticks = base + chunks + hop * (sections - 1)
    plan = Plan(hop, chunks, per_row, sections)
    message = jax.ShapeDtypeStruct((chunk_rows, width), bf16)
    forward_sent, backward_sent = {}, {}
    chunk_flops = 2**10

    for t in range(ticks):
        if t < chunks + hop * (sections - 1):
            sent, info, held, hs, nh = call(
                functools.partial(forward_kernel, plan),
                [message],
                [forward_sent.pop(t - hop, blank), w1, w2, vec, msk],
                info,
                [held, hs, nh],
                forward_scratch(chunk_rows, width, hidden),
                chunk_flops,
                "forward_chunk",
            )
            pairs = [(s, s + 1) for s in range(sections - 1) if 0 <= t - hop * s < chunks]
            if pairs:
                forward_sent[t] = lax.ppermute(sent, "section", pairs)
        if t >= base:
            sent, info, held, vacc, wc, gh = call(
                functools.partial(backward_kernel, plan),
                [message],
                [backward_sent.pop(t - hop, blank), w1, w2, vec, msk],
                info,
                [held, vacc, wc, gh],
                backward_scratch(chunk_rows, width),
                chunk_flops,
                "backward_chunk",
            )
            pairs = [
                (s, s - 1) for s in range(1, sections) if 0 <= t - base - hop * (sections - 1 - s) < chunks
            ]
            if pairs:
                backward_sent[t] = lax.ppermute(sent, "section", pairs)
            info, held, dw1, dw2 = call(
                functools.partial(weight_kernel, plan, unit_chunks),
                [],
                [],
                info,
                [held, dw1, dw2],
                [],
                chunk_flops * unit_chunks,
                "weight_terms",
            )
    grad_scale = (row_count * dp_count * seq_length) ** (-0.5)
    outs, grads, first, second, vectors = pl.pallas_call(
        finish_kernel,
        out_shape=(
            jax.ShapeDtypeStruct((tokens, width), bf16),
            jax.ShapeDtypeStruct((tokens, width), bf16),
            jax.ShapeDtypeStruct((width, ff), bf16),
            jax.ShapeDtypeStruct((width, ff), bf16),
            jax.ShapeDtypeStruct((1, vector_width), f32),
        ),
        in_specs=[pl.BlockSpec(memory_space=VMEM)] * 4,
        out_specs=(
            pl.BlockSpec(memory_space=pltpu.HBM),
            pl.BlockSpec(memory_space=pltpu.HBM),
            pl.BlockSpec(memory_space=VMEM),
            pl.BlockSpec(memory_space=VMEM),
            pl.BlockSpec(memory_space=VMEM),
        ),
        scratch_shapes=[pltpu.SemaphoreType.DMA((2,))],
        compiler_params=params(vmem_mib),
        name="finish",
    )(*(resident(v) for v in (held, dw1, dw2, vacc)))
    share1 = lax.psum_scatter(first, "dp", scatter_dimension=0, tiled=True)
    share2 = lax.psum_scatter(second, "dp", scatter_dimension=1, tiled=True)
    share3 = lax.psum_scatter(vectors[0], "dp", scatter_dimension=0, tiled=True)
    return (
        outs.reshape(1, row_count, seq_length, width),
        grads.reshape(1, row_count, seq_length, width),
        (share1.astype(f32) * grad_scale)[None],
        (share2.astype(f32).T * grad_scale)[None],
        (share3 * grad_scale)[None],
    )


def solution(mesh):
    in_specs = (
        P("dp", None, None),
        P("dp", None),
        P("section", None, None),
        P("section", None, None),
        P("section", None),
        P("dp", None, None),
    )
    out_specs = (
        P("section", "dp", None, None),
        P("section", "dp", None, None),
        P("section", "dp", None),
        P("section", "dp", None),
        P("section", "dp"),
    )
    return jax.shard_map(body, mesh=mesh, in_specs=in_specs, out_specs=out_specs, check_vma=False)
```

```python
import functools
import typing

import jax
import jax.numpy as jnp
from jax import lax
from jax.experimental import pallas as pl
from jax.experimental.pallas import tpu as pltpu
from jax.sharding import PartitionSpec as P

norm_eps = 1e-05
chunk_rows = 256
hop_ticks = 2
lane_block = 256
tall = 64
vmem_mib = 8
f32 = jnp.float32
bf16 = jnp.bfloat16
VMEM = pltpu.VMEM


def resident(array):
    return pltpu.with_memory_space_constraint(array, VMEM)


def nn(left, right):
    return jnp.dot(left, right, preferred_element_type=f32)


def tn(left, right):
    return lax.dot_general(left, right, (((0,), (0,)), ((), ())), preferred_element_type=f32)


def nt(left, right):
    return lax.dot_general(left, right, (((1,), (1,)), ((), ())), preferred_element_type=f32)


def logistic(v):
    return pl.reciprocal(1.0 + jnp.exp(-v), approx=True)


def by_eight(v):
    return jnp.sum(v.reshape(v.shape[0] // 8, 8, v.shape[1]), axis=0)


def span(base, step, size):
    if isinstance(base, int) and isinstance(step, int):
        return slice(base + step, base + step + size)
    return pl.ds(pl.multiple_of(base + step, 128), size)


def doubled(v, axis=0):
    return jnp.concatenate([v, v], axis=axis)


def place_of(shape):
    return lax.broadcasted_iota(jnp.int32, shape, 0)


def across(run, prod, carry, backward):
    place = place_of(run.shape)
    for d in (1, 2, 4):
        seen = place < 8 - d if backward else place >= d
        shift = 8 - d if backward else d
        prod_before = jnp.where(seen, pltpu.roll(prod, shift, 0), 1.0)
        run_before = jnp.where(seen, pltpu.roll(run, shift, 0), 0.0)
        run = run + prod * run_before
        prod = prod * prod_before
    ends = run + prod * carry
    if backward:
        return jnp.where(place < 7, pltpu.roll(ends, 7, 0), carry), ends[0:1, :]
    return jnp.where(place >= 1, pltpu.roll(ends, 1, 0), carry), ends[7:8, :]


def norm_factor(x):
    return lax.rsqrt(jnp.mean(x * x, axis=-1, keepdims=True) + norm_eps)


class Columns(typing.NamedTuple):
    stream: int
    normed: int
    left: int
    grad: int
    outs: int
    sent: int
    wide_a: int
    wide_b: int
    end: int


def columns(width, ff):
    return Columns(*(width * i for i in range(7)), 6 * width + ff, 6 * width + 2 * ff)


class Plan(typing.NamedTuple):
    hop: int
    chunks: int
    per_row: int
    sections: int


def forward_turn(plan, info):
    c = info[2] - plan.hop * info[0]
    return jnp.clip(c, 0, plan.chunks - 1), (c >= 0) & (c < plan.chunks)


def backward_turn(plan, info):
    j = info[3] - plan.hop * (plan.sections - 1 - info[0])
    return jnp.clip(j, 0, plan.chunks - 1), (j >= 0) & (j < plan.chunks)


def backward_chunk(plan, j):
    behind = lax.rem(j, plan.per_row)
    return j - behind + plan.per_row - 1 - behind


def loop(count, step):
    lax.fori_loop(0, count, lambda i, carry: (step(i), carry)[1], 0)


def unrolled(count, step):
    for b in range(count):
        step(b)


def into_runs(held, start, rows_now, column, width, p_s):
    runs = rows_now // 8

    def step(k):
        cols = span(column, 128 * k, 128)
        p_s[:, 0:128] = held[pl.ds(start, rows_now), cols].astype(f32)
        for m in range(rows_now // 16):
            pair = [p_s[pl.ds(2 * m + h, 8, stride=runs), :] for h in (0, 1)]
            held[pl.ds(pl.multiple_of(start + 16 * m, 16), 16), cols] = jnp.concatenate(pair, axis=0).astype(bf16)

    unrolled(width // 128, step)


def forward_kernel(
    plan, recv, w1, w2, vec, msk,
    sc_in, held_in, hs_in, nh_in, send, sc, held, hs, nh,
    pm, p_s, q_s, g_s, nx, kp, mg,
):
    rows_now, width = recv.shape
    ff = w1.shape[1]
    hidden = ff // 2
    col = columns(width, ff)
    c, active = forward_turn(plan, sc)
    start = pl.multiple_of(c * rows_now, rows_now)
    rows = pl.ds(start, rows_now)
    mixer = sc[1] == 0
    tail = width + ff
    tiles = rows_now // 16
    narrow = lambda base: slice(base, base + width)

    def at(r, size):
        return pl.ds(pl.multiple_of(start + r, 16), size)

    @pl.when(active & (sc[0] > 0))
    def _():
        held[rows, narrow(col.stream)] = recv[...]

    @pl.when(active & (sc[0] == 0))
    def _():
        into_runs(held, start, rows_now, col.stream, width, pm)

    @pl.when(active & mixer)
    def _():
        gain = vec[:, :width]

        def norm_step(i):
            here = at(tall * i, tall)
            x = held[here, narrow(col.stream)].astype(f32)
            normed = x * norm_factor(x) * gain
            nx[pl.ds(pl.multiple_of(24 + tall * i, 8), tall), :] = normed
            held[here, narrow(col.normed)] = normed.astype(bf16)
            kp[pl.ds(pl.multiple_of(tall * i, 8), tall), :] = jnp.broadcast_to(msk[here, 0:1], (tall, 128))

        loop(rows_now // tall, norm_step)
        place = place_of((8, width))
        for g in range(0, 24, 8):
            rolled = pltpu.roll(nx[rows_now + g : rows_now + g + 8, :], 1, 0)
            nx[g : g + 8, :] = jnp.where(place == 0, nh[g : g + 8, :], rolled)
            nh[g : g + 8, :] = rolled

        def conv_step(i):
            here = at(tall * i, tall)
            conv = nx[pl.ds(pl.multiple_of(24 + tall * i, 8), tall), :] * vec[:, width : 2 * width]
            for j in range(1, ff // width):
                tap = vec[:, (1 + j) * width : (2 + j) * width]
                earlier = nx[pl.ds(pl.multiple_of(24 - 8 * j + tall * i, 8), tall), :]
                conv = conv + earlier * (msk[here, j - 1 : j] * tap)
            held[here, narrow(col.left)] = conv.astype(bf16)

        loop(rows_now // tall, conv_step)

        def hidden_step(b):
            own = span(0, lane_block * b, lane_block)
            conv16 = held[rows, narrow(col.left)]
            p_s[...] = nn(conv16, w1[:, own])
            q_s[...] = nn(conv16, w1[:, span(hidden, lane_block * b, lane_block)])
            g_s[...] = nt(held[rows, narrow(col.normed)], w2[span(hidden, lane_block * b, lane_block), :])
            bias = vec[:, span(tail, lane_block * b, lane_block)]
            run = prod = None
            for m in range(tiles):
                r = 16 * m
                update = logistic(p_s[r : r + 16, :] + bias)
                candidate = q_s[r : r + 16, :]
                held[at(r, 16), span(col.wide_a, lane_block * b, lane_block)] = update.astype(bf16)
                held[at(r, 16), span(col.wide_a + hidden, lane_block * b, lane_block)] = candidate.astype(bf16)
                decay = (1.0 - update) * doubled(kp[r : r + 16, :], 1)
                fresh = update * candidate
                for h in (0, 8):
                    a, v = decay[h : h + 8, :], fresh[h : h + 8, :]
                    run, prod = (v, a) if run is None else (a * run + v, prod * a)
                    p_s[r + h : r + h + 8, :] = prod
                    q_s[r + h : r + h + 8, :] = run
            inward, last = across(run, prod, hs[0:1, own], False)
            hs[0:1, own] = last
            inward = doubled(inward)
            for m in range(tiles):
                r = 16 * m
                states = q_s[r : r + 16, :] + p_s[r : r + 16, :] * inward
                gate = g_s[r : r + 16, :]
                held[at(r, 16), span(col.wide_b, lane_block * b, lane_block)] = states.astype(bf16)
                held[at(r, 16), span(col.wide_b + hidden, lane_block * b, lane_block)] = gate.astype(bf16)
                mg[r : r + 16, own] = (states * gate * logistic(gate)).astype(bf16)

        unrolled(hidden // lane_block, hidden_step)

        def out_step(b):
            own = span(0, lane_block * b, lane_block)
            x = held[rows, span(col.stream, lane_block * b, lane_block)].astype(f32)
            result = (x + nn(mg[...], w2[:hidden, own])).astype(bf16)
            send[:, own] = result
            held[rows, span(col.outs, lane_block * b, lane_block)] = result

        unrolled(width // lane_block, out_step)

    @pl.when(active & jnp.logical_not(mixer))
    def _():
        gain = vec[:, :width]

        def norm_step(i):
            here = at(tall * i, tall)
            x = held[here, narrow(col.stream)].astype(f32)
            held[here, narrow(col.left)] = (x * norm_factor(x) * gain).astype(bf16)

        loop(rows_now // tall, norm_step)

        norm16 = held[rows, narrow(col.left)]
        for lo in range(0, ff, 256):
            hi = lo + 256
            h = nn(norm16, w1[:, lo:hi]) + vec[:, width + lo : width + hi]
            inner = h * (0.7978845608 + (0.7978845608 * 0.044715) * (h * h))
            half = 0.5 * h
            held[rows, col.wide_a + lo : col.wide_a + hi] = h.astype(bf16)
            held[rows, col.wide_b + lo : col.wide_b + hi] = (half + half * jnp.tanh(inner)).astype(bf16)

        down = nn(held[rows, col.wide_b : col.end], w2[...])
        held[rows, narrow(col.normed)] = down.astype(bf16)
        x = held[rows, narrow(col.stream)].astype(f32)
        result = (x + (down * vec[:, tail : tail + width] + vec[:, tail + width : tail + 2 * width])).astype(bf16)
        send[...] = result
        held[rows, narrow(col.outs)] = result

    sc[2] = sc[2] + 1


def norm_backward(x, factor, gain, grad_normed, grads_wide, vacc):
    width = x.shape[1]
    scaled = x * factor
    vacc[:, :width] = vacc[:, :width] + by_eight(grad_normed * scaled)
    e = grad_normed * gain
    level = jnp.mean(e * scaled, axis=-1, keepdims=True)
    return (grads_wide + factor * (e - scaled * level)).astype(bf16)


def backward_kernel(
    plan, recv, w1, w2, vec, msk,
    sc_in, held_in, vacc_in, wc_in, gh_in, send, sc, held, vacc, wc, gh,
    pm, p_s, q_s, e_s, g_s, nx, gx, gn, kp,
):
    rows_now, width = recv.shape
    ff = w1.shape[1]
    hidden = ff // 2
    col = columns(width, ff)
    j, active = backward_turn(plan, sc)
    start = pl.multiple_of(backward_chunk(plan, j) * rows_now, rows_now)
    rows = pl.ds(start, rows_now)
    mixer = sc[1] == 0
    tail = width + ff
    tiles = rows_now // 16
    narrow = lambda base: slice(base, base + width)

    def at(r, size):
        return pl.ds(pl.multiple_of(start + r, 16), size)

    def before(size):
        return pl.ds(pl.multiple_of(jnp.maximum(start - size, 0), 16), size)

    @pl.when(active & (sc[0] < plan.sections - 1))
    def _():
        held[rows, narrow(col.grad)] = recv[...]

    @pl.when(active & (sc[0] == plan.sections - 1))
    def _():
        into_runs(held, start, rows_now, col.grad, width, pm)

    def add(cols, value):
        vacc[:, cols] = vacc[:, cols] + value

    @pl.when(active & mixer)
    def _():
        gain = vec[:, :width]

        def norm_step(i):
            here = at(tall * i, tall)
            x = held[here, narrow(col.stream)].astype(f32)
            nx[pl.ds(pl.multiple_of(24 + tall * i, 8), tall), :] = x * norm_factor(x) * gain
            kp[pl.ds(pl.multiple_of(tall * i, 8), tall), :] = jnp.broadcast_to(msk[here, 0:1], (tall, 128))

        loop(rows_now // tall, norm_step)
        x_before = held[before(32), narrow(col.stream)].astype(f32)[8:32, :]
        n_before = x_before * norm_factor(x_before) * gain
        place = place_of((8, width))
        for g in range(0, 24, 8):
            nx[g : g + 8, :] = pltpu.roll(
                jnp.where(place == 7, n_before[g : g + 8, :], nx[rows_now + g : rows_now + g + 8, :]), 1, 0
            )

        def hidden_step(b):
            own = span(0, lane_block * b, lane_block)
            on = lambda base: span(base, lane_block * b, lane_block)
            g_s[...] = nt(held[rows, narrow(col.grad)], w2[own, :])
            first = held[before(16), on(col.wide_b)].astype(f32)[8:16, :]
            states = held[at(16 * (tiles - 1), 16), on(col.wide_b)].astype(f32)
            first = pltpu.roll(jnp.where(place_of(first.shape) == 7, first, states[8:16, :]), 1, 0)
            run = prod = None
            for m in range(tiles - 1, -1, -1):
                r = 16 * m
                earlier = None
                if m:
                    earlier = held[at(r - 16, 16), on(col.wide_b)].astype(f32)
                behind = jnp.concatenate([earlier[8:16, :] if m else first, states[0:8, :]], axis=0)
                keep = doubled(kp[r : r + 16, :], 1)
                grad_merged = g_s[r : r + 16, :]
                gate = held[at(r, 16), on(col.wide_b + hidden)].astype(f32)
                update = held[at(r, 16), on(col.wide_a)].astype(f32)
                candidate = held[at(r, 16), on(col.wide_a + hidden)].astype(f32)
                sig = logistic(gate)
                act = gate * sig
                held[at(r, 16), on(col.wide_b)] = (states * act).astype(bf16)
                slope = sig + act * (1.0 - sig)
                held[at(r, 16), on(col.wide_b + hidden)] = (grad_merged * states * slope).astype(bf16)
                left = 1.0 - update
                e_s[r : r + 16, :] = update * left * (candidate - keep * behind)
                decay = left * keep
                grad_states = grad_merged * act
                for h in (8, 0):
                    a, v = decay[h : h + 8, :], grad_states[h : h + 8, :]
                    if run is None:
                        q_s[r + h : r + h + 8, :] = v
                        p_s[r + h : r + h + 8, :] = jnp.ones_like(v)
                        run, prod = a * v, a
                    else:
                        v = v + run
                        q_s[r + h : r + h + 8, :] = v
                        p_s[r + h : r + h + 8, :] = prod
                        run, prod = a * v, prod * a
                states = earlier
            inward, last = across(run, prod, wc[0:1, own], True)
            wc[0:1, own] = last
            inward = doubled(inward)
            total = jnp.zeros((8, lane_block), f32)
            for m in range(tiles):
                r = 16 * m
                carried = q_s[r : r + 16, :] + p_s[r : r + 16, :] * inward
                update = held[at(r, 16), on(col.wide_a)].astype(f32)
                up16 = (carried * e_s[r : r + 16, :]).astype(bf16)
                held[at(r, 16), on(col.wide_a)] = up16
                held[at(r, 16), on(col.wide_a + hidden)] = (carried * update).astype(bf16)
                up = up16.astype(f32)
                total = total + (up[0:8, :] + up[8:16, :])
            add(on(tail), total)

        unrolled(hidden // lane_block, hidden_step)

        def product_step(b):
            own = span(0, lane_block * b, lane_block)
            gx[0:rows_now, own] = nt(held[rows, col.wide_a : col.wide_b], w1[own, :])
            gn[:, own] = nn(held[rows, col.wide_b + hidden : col.end], w2[hidden:, own])

        unrolled(width // lane_block, product_step)
        for g in range(0, 24, 8):
            rolled = pltpu.roll(gx[g : g + 8, :], 7, 0)
            gx[rows_now + g : rows_now + g + 8, :] = jnp.where(place == 7, gh[g : g + 8, :], rolled)
            gh[g : g + 8, :] = rolled

        def out_step(i):
            here = at(tall * i, tall)
            x = held[here, narrow(col.stream)].astype(f32)
            factor = norm_factor(x)
            base = tall * i
            grad_conv = gx[pl.ds(pl.multiple_of(base, 8), tall), :]
            grad_normed = gn[pl.ds(pl.multiple_of(base, 8), tall), :] + vec[:, width : 2 * width] * grad_conv
            add(slice(width, 2 * width), by_eight(grad_conv * nx[pl.ds(pl.multiple_of(24 + base, 8), tall), :]))
            for k in range(1, ff // width):
                cols = slice((1 + k) * width, (2 + k) * width)
                ahead = gx[pl.ds(pl.multiple_of(base + 8 * k, 8), tall), :]
                grad_normed = grad_normed + ahead * (vec[:, cols] * msk[here, 2 + k : 3 + k])
                earlier = nx[pl.ds(pl.multiple_of(24 - 8 * k + base, 8), tall), :]
                add(cols, by_eight(grad_conv * (earlier * msk[here, k - 1 : k])))
            grads_wide = held[here, narrow(col.grad)].astype(f32)
            result = norm_backward(x, factor, gain, grad_normed, grads_wide, vacc)
            send[pl.ds(pl.multiple_of(base, 16), tall), :] = result
            held[here, narrow(col.sent)] = result

        loop(rows_now // tall, out_step)

    @pl.when(active & jnp.logical_not(mixer))
    def _():
        gain = vec[:, :width]

        def scale_step(i):
            here = at(tall * i, tall)
            grads_wide = held[here, narrow(col.grad)].astype(f32)
            down = held[here, narrow(col.normed)].astype(f32)
            add(slice(tail, tail + width), by_eight(grads_wide * down))
            add(slice(tail + width, tail + 2 * width), by_eight(grads_wide))
            held[here, narrow(col.normed)] = (grads_wide * vec[:, tail : tail + width]).astype(bf16)

        loop(rows_now // tall, scale_step)

        def hidden_step(b):
            for u in range(1):
                at_b = 1 * lane_block * b + u * lane_block
                on = lambda base: span(base, at_b, lane_block)
                grad_active = nt(held[rows, narrow(col.normed)], w2[on(0), :])
                h = held[rows, on(col.wide_a)].astype(f32)
                square = h * h
                bend = jnp.tanh(h * (0.7978845608 + (0.7978845608 * 0.044715) * square))
                slope = (0.5 + 0.5 * bend) + (h * (1.0 - bend * bend)) * (
                    0.5 * 0.7978845608 + (0.5 * 0.7978845608 * 3.0 * 0.044715) * square
                )
                hid16 = (grad_active * slope).astype(bf16)
                held[rows, on(col.wide_a)] = hid16
                add(on(width), by_eight(hid16.astype(f32)))

        unrolled(ff // (lane_block * 1), hidden_step)

        def product_step(b):
            own = span(0, lane_block * b, lane_block)
            gn[:, own] = nt(held[rows, col.wide_a : col.wide_b], w1[own, :])

        unrolled(width // lane_block, product_step)

        def out_step(i):
            here = at(tall * i, tall)
            x = held[here, narrow(col.stream)].astype(f32)
            grads_wide = held[here, narrow(col.grad)].astype(f32)
            grad_normed = gn[pl.ds(pl.multiple_of(tall * i, 8), tall), :]
            result = norm_backward(x, norm_factor(x), gain, grad_normed, grads_wide, vacc)
            send[pl.ds(pl.multiple_of(tall * i, 16), tall), :] = result
            held[here, narrow(col.sent)] = result

        loop(rows_now // tall, out_step)


def weight_kernel(
    plan, rows_now, sc_in, held_in, dw1_in, dw2_in, sc, held, dw1, dw2,
):
    width, ff = dw1.shape
    hidden = ff // 2
    col = columns(width, ff)
    j, active = backward_turn(plan, sc)
    rows = pl.ds(pl.multiple_of(backward_chunk(plan, j) * rows_now, rows_now), rows_now)

    def terms(ref, left, right, count, into):
        block = 512
        for lo in range(0, count, block):
            term = tn(left, held[rows, right + lo : right + lo + block])
            cols = slice(into + lo, into + lo + block)
            ref[:, cols] = ref[:, cols] + term

    @pl.when((sc[0] == 0) & (sc[3] == 0))
    def _():
        dw1[...] = jnp.zeros_like(dw1)
        dw2[...] = jnp.zeros_like(dw2)

    @pl.when(active)
    def _():
        terms(dw1, held[rows, col.left : col.left + width], col.wide_a, ff, 0)
        upper = jnp.where(sc[1] == 0, col.grad, col.normed)
        terms(dw2, held[rows, span(upper, 0, width)], col.wide_b, hidden, 0)
        terms(dw2, held[rows, col.normed : col.normed + width], col.wide_b + hidden, hidden, hidden)

    sc[3] = sc[3] + 1


def load_kernel(sections, x_hbm, g_hbm, w1_hbm, w2_hbm, vec_hbm, msk_hbm,
                info, held, w1, w2, vec, msk, hs, nh, wc, gh, vacc, dw1, dw2, blank, sems):
    width, ff = w1.shape
    col = columns(width, ff)
    section = lax.axis_index("section")
    info[0] = section
    info[1] = lax.rem(section, 2)
    info[2] = 0
    info[3] = 0
    moves = [(w1_hbm, w1), (w2_hbm, w2), (vec_hbm, vec), (msk_hbm, msk)]
    copies = [pltpu.make_async_copy(a, b, sems.at[i]) for i, (a, b) in enumerate(moves)]
    first = pltpu.make_async_copy(x_hbm, held.at[:, col.stream : col.stream + width], sems.at[4])
    last = pltpu.make_async_copy(g_hbm, held.at[:, col.grad : col.grad + width], sems.at[5])
    for copy in copies:
        copy.start()

    @pl.when(section == 0)
    def _():
        first.start()

    @pl.when(section == sections - 1)
    def _():
        last.start()

    for ref in (hs, nh, wc, gh, vacc, blank):
        ref[...] = jnp.zeros_like(ref)

    @pl.when(section > 0)
    def _():
        dw1[...] = jnp.zeros_like(dw1)
        dw2[...] = jnp.zeros_like(dw2)

    for copy in copies:
        copy.wait()

    @pl.when(section == 0)
    def _():
        first.wait()

    @pl.when(section == sections - 1)
    def _():
        last.wait()


def piece_of(dw1, dw2, total, owner, owners):
    width, ff = dw1.shape
    high, broad = width // owners, ff // owners
    count = ff // broad
    low = width // count
    yield 0, high, dw1[pl.ds(pl.multiple_of(high * owner, 8), high), :]
    yield high, 16, total
    cols = span(0, broad * owner, broad)
    parts = [dw2[low * q : low * (q + 1), cols] for q in range(count)]
    yield high + 16, low, jnp.concatenate(parts, axis=1)


def total_of(vacc, ff):
    line = jnp.sum(vacc[...], axis=0, keepdims=True)
    rest = line.shape[1] - ff
    second = jnp.concatenate([line[:, ff:], jnp.zeros((1, ff - rest), f32)], axis=1)
    return jnp.concatenate([line[:, :ff], second, jnp.zeros((14, ff), f32)], axis=0)


def finish_kernel(owners, held, dw1, dw2, vacc, outs_out, grads_out, give, sems):
    width, ff = dw1.shape
    col = columns(width, ff)
    copies = [
        pltpu.make_async_copy(held.at[:, base : base + width], target, sems.at[i])
        for i, (base, target) in enumerate(((col.outs, outs_out), (col.sent, grads_out)))
    ]
    for copy in copies:
        copy.start()
    other = 1 - lax.rem(lax.axis_index("dp"), 2)
    total = total_of(vacc, ff)

    def step(z):
        for at, size, value in piece_of(dw1, dw2, total, 2 * z + other, owners):
            give[z, at : at + size, :] = value.astype(bf16)

    loop(owners // 2, step)
    for copy in copies:
        copy.wait()


def share_kernel(owners, dw1, dw2, vacc, got, own, *sends):
    place = lax.axis_index("dp")
    core, chip = lax.rem(place, 2), lax.div(place, 2)
    total = total_of(vacc, dw1.shape[1])
    for ahead, ref in enumerate((own, *sends)):
        z = lax.rem(chip + ahead, owners // 2)
        for at, size, value in piece_of(dw1, dw2, total, 2 * z + core, owners):
            ref[at : at + size, :] = (value + got[z, at : at + size, :].astype(f32)).astype(ref.dtype)


def close_kernel(scale, own, *refs):
    received, (first, second, vectors) = refs[:-3], refs[-3:]
    high = first.shape[0]
    sums = own[...]
    for ref in received:
        sums = sums + ref[...].astype(f32)
    sums = sums * scale
    first[...] = sums[0:high, :]
    vectors[...] = sums[high : high + 8, :]
    broad, width = second.shape
    low = sums.shape[0] - high - 16
    for q in range(width // low):
        second[:, low * q : low * (q + 1)] = sums[high + 16 :, broad * q : broad * (q + 1)].T


def results_kernel(rows_now, outs_in, grads_in, outs_out, grads_out, pm, fetched, stage, in_sems, out_sems):
    runs = rows_now // 8
    tokens, width = outs_in.shape
    chunks = tokens // rows_now

    for source, target in ((outs_in, outs_out), (grads_in, grads_out)):

        def there(c):
            return pl.ds(pl.multiple_of(c * rows_now, rows_now), rows_now)

        def bring(c, slot):
            return pltpu.make_async_copy(source.at[there(c), :], fetched.at[slot], in_sems.at[slot])

        def send(c, slot):
            return pltpu.make_async_copy(stage.at[slot], target.at[there(c), :], out_sems.at[slot])

        bring(0, 0).start()

        def step(c):
            slot = lax.rem(c, 2)

            @pl.when(c + 1 < chunks)
            def _():
                bring(c + 1, 1 - slot).start()

            @pl.when(c >= 2)
            def _():
                send(c - 2, slot).wait()

            bring(c, slot).wait()
            for k in range(width // 128):
                cols = slice(128 * k, 128 * (k + 1))
                for m in range(rows_now // 16):
                    pair = fetched[slot, 16 * m : 16 * m + 16, cols].astype(f32)
                    for h in (0, 1):
                        pm[k, pl.ds(2 * m + h, 8, stride=runs), :] = pair[8 * h : 8 * h + 8, :]
                stage[slot, :, cols] = pm[k].astype(bf16)
            send(c, slot).start()

        loop(chunks, step)
        for c in range(max(0, chunks - 2), chunks):
            send(c, c % 2).wait()


def forward_scratch(rows, width, hidden):
    return (
        [VMEM((rows, 128), f32)]
        + [VMEM((rows, lane_block), f32)] * 3
        + [VMEM((rows + 24, width), f32), VMEM((rows, 128), f32), VMEM((rows, hidden), bf16)]
    )


def backward_scratch(rows, width):
    return (
        [VMEM((rows, 128), f32)]
        + [VMEM((rows, lane_block), f32)] * 4
        + [VMEM((rows + 24, width), f32)] * 2
        + [VMEM((rows, width), f32), VMEM((rows, 128), f32)]
    )


def params():
    return pltpu.CompilerParams(vmem_limit_bytes=vmem_mib * 2**20)


def call(kernel, plain_out, inputs, info, state, scratch, flops, name):
    kept = (pltpu.SMEM(info.shape, info.dtype),) + tuple(VMEM(s.shape, s.dtype) for s in state)
    kept_specs = [pl.BlockSpec(memory_space=pltpu.SMEM)] + [pl.BlockSpec(memory_space=VMEM) for _ in state]
    return pl.pallas_call(
        kernel,
        out_shape=tuple(plain_out) + kept,
        in_specs=[pl.BlockSpec(memory_space=VMEM) for _ in inputs] + kept_specs,
        out_specs=tuple([pl.BlockSpec(memory_space=VMEM) for _ in plain_out] + kept_specs),
        input_output_aliases={len(inputs) + i: len(plain_out) + i for i in range(len(kept))},
        scratch_shapes=scratch,
        compiler_params=params(),
        cost_estimate=pl.CostEstimate(flops=flops, bytes_accessed=0, transcendentals=0),
        name=name,
    )(*inputs, info, *state)


def body(layer_input, resets, first_weights, second_weights, section_vectors, cotangent):
    row_count, seq_length, width = layer_input.shape
    ff = first_weights.shape[2]
    hidden = ff // 2
    vector_width = section_vectors.shape[1]
    section = lax.axis_index("section")
    sections = lax.axis_size("section")
    dp_count = lax.axis_size("dp")
    tokens = row_count * seq_length
    per_row = seq_length // chunk_rows
    chunks = row_count * per_row

    keep = 1.0 - resets.astype(f32)
    keep = jnp.concatenate([jnp.zeros((row_count, 1), f32), keep[:, 1:]], axis=1).reshape(-1)

    def later(v, j):
        return jnp.concatenate([jnp.zeros((j,), f32), v[:-j]])

    def sooner(v, j):
        return jnp.concatenate([v[j:], jnp.zeros((j,), f32)])

    m1 = keep
    m2 = keep * later(keep, 1)
    m3 = m2 * later(keep, 2)
    msk = jnp.stack([m1, m2, m3, sooner(m1, 1), sooner(m2, 2), sooner(m3, 3), m1, m1], axis=1)
    msk = msk.reshape(chunks, 8, chunk_rows // 8, 8).swapaxes(1, 2).reshape(tokens, 8)


    made = (
        pltpu.SMEM((4,), jnp.int32), VMEM((tokens, 6 * width + 2 * ff), bf16),
        VMEM((width, ff), bf16), VMEM((ff, width), bf16), VMEM((1, vector_width), f32), VMEM(msk.shape, f32),
        VMEM((8, hidden), f32), VMEM((24, width), f32), VMEM((8, hidden), f32), VMEM((24, width), f32),
        VMEM((8, vector_width), f32), VMEM((width, ff), f32), VMEM((width, ff), f32),
        VMEM((chunk_rows, width), bf16),
    )
    inputs = [
        layer_input.reshape(tokens, width), cotangent.reshape(tokens, width),
        first_weights[0], second_weights[0], section_vectors, msk,
    ]
    info, held, w1, w2, vec, msk, hs, nh, wc, gh, vacc, dw1, dw2, blank = pl.pallas_call(
        functools.partial(load_kernel, sections),
        out_shape=made,
        in_specs=[pl.BlockSpec(memory_space=pltpu.HBM)] * 6,
        out_specs=(pl.BlockSpec(memory_space=pltpu.SMEM),) + tuple(pl.BlockSpec(memory_space=VMEM) for _ in made[1:]),
        scratch_shapes=[pltpu.SemaphoreType.DMA((6,))],
        compiler_params=params(),
        name="load",
    )(
        *(pltpu.with_memory_space_constraint(v, pltpu.HBM) for v in inputs),
    )
    w1, w2, vec, msk = (resident(v) for v in (w1, w2, vec, msk))

    hop = hop_ticks
    base = per_row - 1 + hop * (sections - 1)
    ticks = base + chunks + hop * (sections - 1)
    plan = Plan(hop, chunks, per_row, sections)
    message = jax.ShapeDtypeStruct((chunk_rows, width), bf16)
    forward_sent, backward_sent = {}, {}
    chunk_flops = 2**10

    for t in range(ticks):
        if t < chunks + hop * (sections - 1):
            sent, info, held, hs, nh = call(
                functools.partial(forward_kernel, plan),
                [message],
                [forward_sent.pop(t - hop, blank), w1, w2, vec, msk],
                info,
                [held, hs, nh],
                forward_scratch(chunk_rows, width, hidden),
                chunk_flops,
                "forward_chunk",
            )
            pairs = [(s, s + 1) for s in range(sections - 1) if 0 <= t - hop * s < chunks]
            if pairs:
                forward_sent[t] = lax.ppermute(sent, "section", pairs)
        if t >= base:
            sent, info, held, vacc, wc, gh = call(
                functools.partial(backward_kernel, plan),
                [message],
                [backward_sent.pop(t - hop, blank), w1, w2, vec, msk],
                info,
                [held, vacc, wc, gh],
                backward_scratch(chunk_rows, width),
                chunk_flops,
                "backward_chunk",
            )
            pairs = [
                (s, s - 1) for s in range(1, sections) if 0 <= t - base - hop * (sections - 1 - s) < chunks
            ]
            if pairs:
                backward_sent[t] = lax.ppermute(sent, "section", pairs)
            info, held, dw1, dw2 = call(
                functools.partial(weight_kernel, plan, chunk_rows),
                [],
                [],
                info,
                [held, dw1, dw2],
                [],
                chunk_flops,
                "weight_terms",
            )
    owners = dp_count if dp_count == 8 else 2
    piece = (width // owners + 16 + width // owners, ff)
    vmem_spec, hbm_spec = pl.BlockSpec(memory_space=VMEM), pl.BlockSpec(memory_space=pltpu.HBM)
    flat = jax.ShapeDtypeStruct((tokens, width), bf16)
    raw_outs, raw_grads, give = pl.pallas_call(
        functools.partial(finish_kernel, owners),
        out_shape=(flat, flat, jax.ShapeDtypeStruct((owners // 2, *piece), bf16)),
        in_specs=[vmem_spec] * 4,
        out_specs=(hbm_spec, hbm_spec, vmem_spec),
        scratch_shapes=[pltpu.SemaphoreType.DMA((2,))],
        compiler_params=params(),
        name="finish",
    )(*(resident(v) for v in (held, dw1, dw2, vacc)))
    scale = (row_count * dp_count * seq_length) ** (-0.5)
    if owners == dp_count:
        got = lax.ppermute(give, "dp", [(d, d ^ 1) for d in range(dp_count)])
        chips = dp_count // 2
        own, *sends = pl.pallas_call(
            functools.partial(share_kernel, owners),
            out_shape=(jax.ShapeDtypeStruct(piece, f32),) + (jax.ShapeDtypeStruct(piece, bf16),) * (chips - 1),
            in_specs=[vmem_spec] * 4,
            out_specs=(vmem_spec,) * chips,
            compiler_params=params(),
            name="share",
        )(*(resident(v) for v in (dw1, dw2, vacc)), got)
        received = [
            lax.ppermute(sent, "dp", [(d, (d + 2 * ahead) % dp_count) for d in range(dp_count)])
            for ahead, sent in zip(range(1, chips), sends)
        ]
        first, second, vectors = pl.pallas_call(
            functools.partial(close_kernel, scale),
            out_shape=(
                jax.ShapeDtypeStruct((width // owners, ff), f32),
                jax.ShapeDtypeStruct((ff // owners, width), f32),
                jax.ShapeDtypeStruct((8, ff), f32),
            ),
            in_specs=[vmem_spec] * chips,
            out_specs=(vmem_spec,) * 3,
            compiler_params=params(),
            name="close",
        )(own, *received)
        line = vectors[:2].reshape(-1)
        part = vector_width // dp_count
        vectors = lax.dynamic_slice_in_dim(line, part * lax.axis_index("dp"), part)
    else:
        first = lax.psum_scatter(dw1.astype(bf16), "dp", scatter_dimension=0, tiled=True).astype(f32) * scale
        second = lax.psum_scatter(dw2.astype(bf16), "dp", scatter_dimension=1, tiled=True).astype(f32).T * scale
        vectors = lax.psum_scatter(jnp.sum(vacc, axis=0), "dp", scatter_dimension=0, tiled=True) * scale
    outs, grads = pl.pallas_call(
        functools.partial(results_kernel, chunk_rows),
        out_shape=(flat, flat),
        in_specs=[hbm_spec] * 2,
        out_specs=(hbm_spec,) * 2,
        scratch_shapes=[
            VMEM((width // 128, chunk_rows, 128), f32),
            VMEM((2, chunk_rows, width), bf16),
            VMEM((2, chunk_rows, width), bf16),
            pltpu.SemaphoreType.DMA((2,)),
            pltpu.SemaphoreType.DMA((2,)),
        ],
        compiler_params=params(),
        cost_estimate=pl.CostEstimate(flops=2**33, bytes_accessed=2**23, transcendentals=0),
        name="results",
    )(*(pltpu.with_memory_space_constraint(v, pltpu.HBM) for v in (raw_outs, raw_grads)))
    return (
        outs.reshape(1, row_count, seq_length, width),
        grads.reshape(1, row_count, seq_length, width),
        first[None],
        second[None],
        vectors[None],
    )


def solution(mesh):
    in_specs = (
        P("dp", None, None),
        P("dp", None),
        P("section", None, None),
        P("section", None, None),
        P("section", None),
        P("dp", None, None),
    )
    out_specs = (
        P("section", "dp", None, None),
        P("section", "dp", None, None),
        P("section", "dp", None),
        P("section", "dp", None),
        P("section", "dp"),
    )
    return jax.shard_map(body, mesh=mesh, in_specs=in_specs, out_specs=out_specs, check_vma=False)
```

```python
import functools
import typing

import jax
import jax.numpy as jnp
from jax import lax
from jax.experimental import pallas as pl
from jax.experimental.pallas import tpu as pltpu
from jax.sharding import PartitionSpec as P

norm_eps = 1e-05
chunk_rows = 256
hop_ticks = 2
lane_block = 256
tall = 64
vmem_mib = 6
f32 = jnp.float32
bf16 = jnp.bfloat16
VMEM = pltpu.VMEM


def resident(array):
    return pltpu.with_memory_space_constraint(array, VMEM)


def nn(left, right):
    return jnp.dot(left, right, preferred_element_type=f32)


def tn(left, right):
    return lax.dot_general(left, right, (((0,), (0,)), ((), ())), preferred_element_type=f32)


def nt(left, right):
    return lax.dot_general(left, right, (((1,), (1,)), ((), ())), preferred_element_type=f32)


def logistic(v):
    return pl.reciprocal(1.0 + jnp.exp(-v), approx=True)


def by_eight(v):
    return jnp.sum(v.reshape(v.shape[0] // 8, 8, v.shape[1]), axis=0)


def span(base, step, size):
    if isinstance(base, int) and isinstance(step, int):
        return slice(base + step, base + step + size)
    return pl.ds(pl.multiple_of(base + step, 128), size)


def lines(first, size, multiple=8):
    if isinstance(first, int):
        return slice(first, first + size)
    return pl.ds(pl.multiple_of(first, multiple), size)


def doubled(v, axis=0):
    return jnp.concatenate([v, v], axis=axis)


def place_of(shape):
    return lax.broadcasted_iota(jnp.int32, shape, 0)


def across(run, prod, carry, backward):
    place = place_of(run.shape)
    for d in (1, 2, 4):
        seen = place < 8 - d if backward else place >= d
        shift = 8 - d if backward else d
        prod_before = jnp.where(seen, pltpu.roll(prod, shift, 0), 1.0)
        run_before = jnp.where(seen, pltpu.roll(run, shift, 0), 0.0)
        run = run + prod * run_before
        prod = prod * prod_before
    ends = run + prod * carry
    if backward:
        return jnp.where(place < 7, pltpu.roll(ends, 7, 0), carry), ends[0:1, :]
    return jnp.where(place >= 1, pltpu.roll(ends, 1, 0), carry), ends[7:8, :]


def norm_factor(x):
    return lax.rsqrt(jnp.mean(x * x, axis=-1, keepdims=True) + norm_eps)


class Columns(typing.NamedTuple):
    stream: int
    normed: int
    left: int
    grad: int
    outs: int
    sent: int
    wide_a: int
    wide_b: int
    slope: int
    end: int


def columns(width, ff):
    wide = 6 * width + 2 * ff
    return Columns(*(width * i for i in range(7)), 6 * width + ff, wide, wide + ff // 2)


class Plan(typing.NamedTuple):
    hop: int
    chunks: int
    per_row: int
    sections: int


def forward_turn(plan, info):
    c = info[2] - plan.hop * info[0]
    return jnp.clip(c, 0, plan.chunks - 1), (c >= 0) & (c < plan.chunks)


def backward_turn(plan, info):
    j = info[3] - plan.hop * (plan.sections - 1 - info[0])
    return jnp.clip(j, 0, plan.chunks - 1), (j >= 0) & (j < plan.chunks)


def backward_chunk(plan, j):
    behind = lax.rem(j, plan.per_row)
    return j - behind + plan.per_row - 1 - behind


def loop(count, step):
    lax.fori_loop(0, count, lambda i, carry: (step(i), carry)[1], 0)


def unrolled(count, step):
    for b in range(count):
        step(b)


def into_runs(held, start, rows_now, column, width, p_s):
    runs = rows_now // 8

    def step(k):
        cols = span(column, 128 * k, 128)
        p_s[:, 0:128] = held[pl.ds(start, rows_now), cols].astype(f32)
        for m in range(rows_now // 16):
            pair = [p_s[pl.ds(2 * m + h, 8, stride=runs), :] for h in (0, 1)]
            held[pl.ds(pl.multiple_of(start + 16 * m, 16), 16), cols] = jnp.concatenate(pair, axis=0).astype(bf16)

    unrolled(width // 128, step)


def forward_kernel(
    plan, recv, w1, w2, vec,
    sc_in, held_in, msk_in, hs_in, nh_in, send, sc, held, msk, hs, nh,
    pm, p_2, q_2, e_2, g_2, nx, kp,
):
    rows_now, width = recv.shape
    ff = w1.shape[1]
    hidden = ff // 2
    col = columns(width, ff)
    c, active = forward_turn(plan, sc)
    start = pl.multiple_of(c * rows_now, rows_now)
    rows = pl.ds(start, rows_now)
    mixer = sc[1] == 0
    tail = width + ff
    tiles = rows_now // 16
    narrow = lambda base: slice(base, base + width)

    def at(r, size):
        return pl.ds(pl.multiple_of(start + r, 16), size)

    @pl.when(active & (sc[0] > 0))
    def _():
        held[rows, narrow(col.stream)] = recv[...]

    @pl.when(active & (sc[0] == 0))
    def _():
        into_runs(held, start, rows_now, col.stream, width, pm)

    @pl.when(active & mixer)
    def _():
        gain = vec[:, :width]

        def norm_step(i):
            here = at(tall * i, tall)
            x = held[here, narrow(col.stream)].astype(f32)
            factor = norm_factor(x)
            normed = x * factor * gain
            nx[lines(24 + tall * i, tall, 8), :] = normed
            held[here, narrow(col.normed)] = normed.astype(bf16)
            msk[here, 6:7] = factor
            kp[lines(tall * i, tall, 8), :] = jnp.broadcast_to(msk[here, 0:1], (tall, 128))

        unrolled(rows_now // tall, norm_step)
        place = place_of((8, width))
        for g in range(0, 24, 8):
            rolled = pltpu.roll(nx[rows_now + g : rows_now + g + 8, :], 1, 0)
            nx[g : g + 8, :] = jnp.where(place == 0, nh[g : g + 8, :], rolled)
            nh[g : g + 8, :] = rolled

        def conv_step(i):
            here = at(tall * i, tall)
            conv = nx[lines(24 + tall * i, tall, 8), :] * vec[:, width : 2 * width]
            for j in range(1, ff // width):
                tap = vec[:, (1 + j) * width : (2 + j) * width]
                earlier = nx[lines(24 - 8 * j + tall * i, tall, 8), :]
                conv = conv + earlier * (msk[here, j - 1 : j] * tap)
            held[here, narrow(col.left)] = conv.astype(bf16)

        unrolled(rows_now // tall, conv_step)

        def hidden_step(b):
            own = span(0, lane_block * b, lane_block)
            conv16 = held[rows, narrow(col.left)]
            p_s, q_s, e_s, g_s = (ref.at[b % 2] for ref in (p_2, q_2, e_2, g_2))
            p_s[...] = nn(conv16, w1[:, own])
            e_s[...] = nn(conv16, w1[:, span(hidden, lane_block * b, lane_block)])
            g_s[...] = nt(held[rows, narrow(col.normed)], w2[span(hidden, lane_block * b, lane_block), :])
            bias = vec[:, span(tail, lane_block * b, lane_block)]
            on = lambda base: span(base, lane_block * b, lane_block)
            run = prod = None
            for m in range(tiles):
                r = 16 * m
                update = logistic(p_s[r : r + 16, :] + bias)
                held[at(r, 16), on(col.wide_a)] = update.astype(bf16)
                decay = (1.0 - update) * doubled(kp[r : r + 16, :], 1)
                fresh = update * e_s[r : r + 16, :]
                for h in (0, 8):
                    a, v = decay[h : h + 8, :], fresh[h : h + 8, :]
                    run, prod = (v, a) if run is None else (a * run + v, prod * a)
                    p_s[r + h : r + h + 8, :] = prod
                    q_s[r + h : r + h + 8, :] = run
            inward, last = across(run, prod, hs[0:1, own], False)
            hs[0:1, own] = last
            inward = doubled(inward)
            for m in range(tiles):
                r = 16 * m
                states = q_s[r : r + 16, :] + p_s[r : r + 16, :] * inward
                gate = g_s[r : r + 16, :]
                sig = logistic(gate)
                act = gate * sig
                held[at(r, 16), on(col.wide_b)] = (states * act).astype(bf16)
                held[at(r, 16), on(col.slope)] = act.astype(bf16)
                held[at(r, 16), on(col.wide_b + hidden)] = (states * (sig + act * (1.0 - sig))).astype(bf16)
                update = held[at(r, 16), on(col.wide_a)].astype(f32)
                held[at(r, 16), on(col.wide_a + hidden)] = (update * (e_s[r : r + 16, :] - states)).astype(bf16)

        unrolled(hidden // lane_block, hidden_step)

        def out_step(b):
            own = span(0, lane_block * b, lane_block)
            x = held[rows, span(col.stream, lane_block * b, lane_block)].astype(f32)
            result = (x + nn(held[rows, col.wide_b : col.wide_b + hidden], w2[:hidden, own])).astype(bf16)
            send[:, own] = result
            held[rows, span(col.outs, lane_block * b, lane_block)] = result

        unrolled(width // lane_block, out_step)

    @pl.when(active & jnp.logical_not(mixer))
    def _():
        gain = vec[:, :width]

        def norm_step(i):
            here = at(tall * i, tall)
            x = held[here, narrow(col.stream)].astype(f32)
            factor = norm_factor(x)
            msk[here, 6:7] = factor
            held[here, narrow(col.left)] = (x * factor * gain).astype(bf16)

        unrolled(rows_now // tall, norm_step)

        norm16 = held[rows, narrow(col.left)]
        for lo in range(0, ff, lane_block):
            hi = lo + lane_block
            h = nn(norm16, w1[:, lo:hi]) + vec[:, width + lo : width + hi]
            square = h * h
            bend = jnp.tanh(h * (0.7978845608 + (0.7978845608 * 0.044715) * square))
            half = 0.5 + 0.5 * bend
            held[rows, col.wide_b + lo : col.wide_b + hi] = (h * half).astype(bf16)
            slope = half + (h * (1.0 - bend * bend)) * (
                0.5 * 0.7978845608 + (0.5 * 0.7978845608 * 3.0 * 0.044715) * square
            )
            held[rows, col.wide_a + lo : col.wide_a + hi] = slope.astype(bf16)
        down = nn(held[rows, col.wide_b : col.slope], w2[...])
        held[rows, narrow(col.normed)] = down.astype(bf16)
        x = held[rows, narrow(col.stream)].astype(f32)
        result = (x + (down * vec[:, tail : tail + width] + vec[:, tail + width : tail + 2 * width])).astype(bf16)
        send[...] = result
        held[rows, narrow(col.outs)] = result

    sc[2] = sc[2] + 1


def norm_backward(x, factor, gain, grad_normed, grads_wide, vacc):
    width = x.shape[1]
    scaled = x * factor
    vacc[:, :width] = vacc[:, :width] + by_eight(grad_normed * scaled)
    e = grad_normed * gain
    level = jnp.mean(e * scaled, axis=-1, keepdims=True)
    return (grads_wide + factor * (e - scaled * level)).astype(bf16)


def backward_kernel(
    plan, recv, w1, w2, vec,
    sc_in, held_in, msk_in, vacc_in, wc_in, gh_in, send, sc, held, msk, vacc, wc, gh,
    pm, p_2, q_2, g_2, nx, gx, gn, kp,
):
    rows_now, width = recv.shape
    ff = w1.shape[1]
    hidden = ff // 2
    col = columns(width, ff)
    j, active = backward_turn(plan, sc)
    start = pl.multiple_of(backward_chunk(plan, j) * rows_now, rows_now)
    rows = pl.ds(start, rows_now)
    mixer = sc[1] == 0
    tail = width + ff
    tiles = rows_now // 16
    narrow = lambda base: slice(base, base + width)

    def at(r, size):
        return pl.ds(pl.multiple_of(start + r, 16), size)

    def before(size):
        return pl.ds(pl.multiple_of(jnp.maximum(start - size, 0), 16), size)

    @pl.when(active & (sc[0] < plan.sections - 1))
    def _():
        held[rows, narrow(col.grad)] = recv[...]

    @pl.when(active & (sc[0] == plan.sections - 1))
    def _():
        into_runs(held, start, rows_now, col.grad, width, pm)

    def add(cols, value):
        vacc[:, cols] = vacc[:, cols] + value

    @pl.when(active & mixer)
    def _():
        gain = vec[:, :width]

        def norm_step(i):
            here = at(tall * i, tall)
            nx[lines(24 + tall * i, tall, 8), :] = held[here, narrow(col.normed)].astype(f32)
            kp[lines(tall * i, tall, 8), :] = jnp.broadcast_to(msk[here, 0:1], (tall, 128))

        unrolled(rows_now // tall, norm_step)
        n_before = held[before(32), narrow(col.normed)].astype(f32)[8:32, :]
        place = place_of((8, width))
        for g in range(0, 24, 8):
            nx[g : g + 8, :] = pltpu.roll(
                jnp.where(place == 7, n_before[g : g + 8, :], nx[rows_now + g : rows_now + g + 8, :]), 1, 0
            )

        def hidden_step(b):
            own = span(0, lane_block * b, lane_block)
            on = lambda base: span(base, lane_block * b, lane_block)
            p_s, q_s, g_s = (ref.at[b % 2] for ref in (p_2, q_2, g_2))
            g_s[...] = nt(held[rows, narrow(col.grad)], w2[own, :])
            run = prod = None
            for m in range(tiles - 1, -1, -1):
                r = 16 * m
                grad_merged = g_s[r : r + 16, :]
                turn = held[at(r, 16), on(col.wide_b + hidden)].astype(f32)
                held[at(r, 16), on(col.wide_b + hidden)] = (grad_merged * turn).astype(bf16)
                update = held[at(r, 16), on(col.wide_a)].astype(f32)
                decay = (1.0 - update) * doubled(kp[r : r + 16, :], 1)
                grad_states = grad_merged * held[at(r, 16), on(col.slope)].astype(f32)
                for h in (8, 0):
                    a, v = decay[h : h + 8, :], grad_states[h : h + 8, :]
                    if run is None:
                        prod = jnp.ones_like(v)
                    else:
                        v = v + run
                    q_s[r + h : r + h + 8, :] = v
                    p_s[r + h : r + h + 8, :] = prod
                    run, prod = a * v, prod * a
            inward, last = across(run, prod, wc[0:1, own], True)
            wc[0:1, own] = last
            inward = doubled(inward)
            total = jnp.zeros((8, lane_block), f32)
            for m in range(tiles):
                r = 16 * m
                carried = q_s[r : r + 16, :] + p_s[r : r + 16, :] * inward
                update = held[at(r, 16), on(col.wide_a)].astype(f32)
                up16 = (carried * held[at(r, 16), on(col.wide_a + hidden)].astype(f32)).astype(bf16)
                held[at(r, 16), on(col.wide_a)] = up16
                held[at(r, 16), on(col.wide_a + hidden)] = (carried * update).astype(bf16)
                up = up16.astype(f32)
                total = total + (up[0:8, :] + up[8:16, :])
            add(on(tail), total)

        unrolled(hidden // lane_block, hidden_step)

        def product_step(b):
            own = span(0, lane_block * b, lane_block)
            gx[0:rows_now, own] = nt(held[rows, col.wide_a : col.wide_b], w1[own, :])
            gn[:, own] = nn(held[rows, col.wide_b + hidden : col.slope], w2[hidden:, own])

        unrolled(width // lane_block, product_step)
        for g in range(0, 24, 8):
            rolled = pltpu.roll(gx[g : g + 8, :], 7, 0)
            gx[rows_now + g : rows_now + g + 8, :] = jnp.where(place == 7, gh[g : g + 8, :], rolled)
            gh[g : g + 8, :] = rolled

        def out_step(i):
            here = at(tall * i, tall)
            x = held[here, narrow(col.stream)].astype(f32)
            factor = msk[here, 6:7]
            base = tall * i
            grad_conv = gx[lines(base, tall, 8), :]
            grad_normed = gn[lines(base, tall, 8), :] + vec[:, width : 2 * width] * grad_conv
            add(slice(width, 2 * width), by_eight(grad_conv * nx[lines(24 + base, tall, 8), :]))
            for k in range(1, ff // width):
                cols = slice((1 + k) * width, (2 + k) * width)
                ahead = gx[lines(base + 8 * k, tall, 8), :]
                grad_normed = grad_normed + ahead * (vec[:, cols] * msk[here, 2 + k : 3 + k])
                earlier = nx[lines(24 - 8 * k + base, tall, 8), :]
                add(cols, by_eight(grad_conv * (earlier * msk[here, k - 1 : k])))
            grads_wide = held[here, narrow(col.grad)].astype(f32)
            result = norm_backward(x, factor, gain, grad_normed, grads_wide, vacc)
            send[lines(base, tall, 16), :] = result
            held[here, narrow(col.sent)] = result

        unrolled(rows_now // tall, out_step)

    @pl.when(active & jnp.logical_not(mixer))
    def _():
        gain = vec[:, :width]

        def scale_step(i):
            here = at(tall * i, tall)
            grads_wide = held[here, narrow(col.grad)].astype(f32)
            down = held[here, narrow(col.normed)].astype(f32)
            add(slice(tail, tail + width), by_eight(grads_wide * down))
            add(slice(tail + width, tail + 2 * width), by_eight(grads_wide))
            held[here, narrow(col.normed)] = (grads_wide * vec[:, tail : tail + width]).astype(bf16)

        unrolled(rows_now // tall, scale_step)

        def hidden_step(b):
            for u in range(1):
                at_b = 1 * lane_block * b + u * lane_block
                on = lambda base: span(base, at_b, lane_block)
                grad_active = nt(held[rows, narrow(col.normed)], w2[on(0), :])
                hid16 = (grad_active * held[rows, on(col.wide_a)].astype(f32)).astype(bf16)
                held[rows, on(col.wide_a)] = hid16
                add(on(width), by_eight(hid16.astype(f32)))

        unrolled(ff // (lane_block * 1), hidden_step)

        def product_step(b):
            own = span(0, lane_block * b, lane_block)
            gn[:, own] = nt(held[rows, col.wide_a : col.wide_b], w1[own, :])

        unrolled(width // lane_block, product_step)

        def out_step(i):
            here = at(tall * i, tall)
            x = held[here, narrow(col.stream)].astype(f32)
            grads_wide = held[here, narrow(col.grad)].astype(f32)
            grad_normed = gn[lines(tall * i, tall, 8), :]
            result = norm_backward(x, msk[here, 6:7], gain, grad_normed, grads_wide, vacc)
            send[lines(tall * i, tall, 16), :] = result
            held[here, narrow(col.sent)] = result

        unrolled(rows_now // tall, out_step)


def weight_kernel(
    plan, rows_now, sc_in, held_in, dw1_in, dw2_in, sc, held, dw1, dw2,
):
    width, ff = dw1.shape
    hidden = ff // 2
    col = columns(width, ff)
    j = sc[3] - plan.hop * (plan.sections - 1)
    active = j >= 0
    rows = pl.ds(pl.multiple_of(backward_chunk(plan, jnp.maximum(j, 0)) * rows_now, rows_now), rows_now)

    def terms(ref, left, right, count, into):
        block = 512
        for lo in range(0, count, block):
            term = tn(left, held[rows, right + lo : right + lo + block])
            cols = slice(into + lo, into + lo + block)
            ref[:, cols] = ref[:, cols] + term

    @pl.when((sc[0] == 0) & (j == -1))
    def _():
        dw1[...] = jnp.zeros_like(dw1)
        dw2[...] = jnp.zeros_like(dw2)

    @pl.when(active)
    def _():
        terms(dw1, held[rows, col.left : col.left + width], col.wide_a, ff, 0)
        upper = jnp.where(sc[1] == 0, col.grad, col.normed)
        terms(dw2, held[rows, span(upper, 0, width)], col.wide_b, hidden, 0)
        terms(dw2, held[rows, col.normed : col.normed + width], col.wide_b + hidden, hidden, hidden)

    sc[3] = sc[3] + 1


def load_kernel(sections, x_hbm, g_hbm, w1_hbm, w2_hbm, vec_hbm, msk_hbm,
                info, held, w1, w2, vec, msk, hs, nh, wc, gh, vacc, dw1, dw2, blank, sems):
    width, ff = w1.shape
    col = columns(width, ff)
    section = lax.axis_index("section")
    info[0] = section
    info[1] = lax.rem(section, 2)
    info[2] = 0
    info[3] = 0
    moves = [(w1_hbm, w1), (w2_hbm, w2), (vec_hbm, vec), (msk_hbm, msk)]
    copies = [pltpu.make_async_copy(a, b, sems.at[i]) for i, (a, b) in enumerate(moves)]
    first = pltpu.make_async_copy(x_hbm, held.at[:, col.stream : col.stream + width], sems.at[4])
    last = pltpu.make_async_copy(g_hbm, held.at[:, col.grad : col.grad + width], sems.at[5])
    for copy in copies:
        copy.start()

    @pl.when(section == 0)
    def _():
        first.start()

    @pl.when(section == sections - 1)
    def _():
        last.start()

    for ref in (hs, nh, wc, gh, vacc, blank):
        ref[...] = jnp.zeros_like(ref)

    @pl.when(section > 0)
    def _():
        dw1[...] = jnp.zeros_like(dw1)
        dw2[...] = jnp.zeros_like(dw2)

    for copy in copies:
        copy.wait()

    @pl.when(section == 0)
    def _():
        first.wait()

    @pl.when(section == sections - 1)
    def _():
        last.wait()


def piece_of(dw1, dw2, owner, owners):
    width, ff = dw1.shape
    high, broad = width // owners, ff // owners
    count = ff // broad
    low = width // count
    yield 0, high, dw1[pl.ds(pl.multiple_of(high * owner, 8), high), :]
    cols = span(0, broad * owner, broad)
    parts = [dw2[low * q : low * (q + 1), cols] for q in range(count)]
    yield high, low, jnp.concatenate(parts, axis=1)


def finish_kernel(owners, held, dw1, dw2, vacc, outs_out, grads_out, give, keep, sems):
    width, ff = dw1.shape
    col = columns(width, ff)
    copies = [
        pltpu.make_async_copy(held.at[:, base : base + width], target, sems.at[i])
        for i, (base, target) in enumerate(((col.outs, outs_out), (col.sent, grads_out)))
    ]
    for copy in copies:
        copy.start()
    core = lax.rem(lax.axis_index("dp"), 2)
    line = jnp.sum(vacc[...], axis=0, keepdims=True)
    lines = line.shape[1] // 128
    total = jnp.concatenate(
        [line[:, 128 * i : 128 * (i + 1)] for i in range(lines)]
        + [jnp.zeros((give.shape[1] - lines, 128), f32)],
        axis=0,
    )

    def step(z):
        for mine, ref in ((core, keep), (1 - core, give)):
            for at, size, value in piece_of(dw1, dw2, 2 * z + mine, owners):
                ref[z, at : at + size, 0:ff] = value.astype(ref.dtype)
            ref[z, :, ff:] = total.astype(ref.dtype)

    loop(owners // 2, step)
    for copy in copies:
        copy.wait()


def raw_kernel(width, ff, held, outs_out, grads_out, sems):
    col = columns(width, ff)
    copies = [
        pltpu.make_async_copy(held.at[:, base : base + width], target, sems.at[i])
        for i, (base, target) in enumerate(((col.outs, outs_out), (col.sent, grads_out)))
    ]
    for copy in copies:
        copy.start()
    for copy in copies:
        copy.wait()


def share_kernel(chips, keep, got, own, *sends):
    chip = lax.div(lax.axis_index("dp"), 2)
    for ahead, ref in enumerate((own, *sends)):
        z = lax.rem(chip + ahead, chips)
        ref[...] = (keep[z] + got[z].astype(f32)).astype(ref.dtype)


def close_kernel(scale, own, *refs):
    received, (first, second, vectors) = refs[:-3], refs[-3:]
    high = first.shape[0]
    sums = own[...]
    for ref in received:
        sums = sums + ref[...].astype(f32)
    sums = sums * scale
    broad, width = second.shape
    low = sums.shape[0] - high
    ff = first.shape[1]
    first[...] = sums[0:high, 0:ff]
    part = vectors.shape[1]
    count = -(-part // 128)
    lines = sums[0 : 8 * (-(-(len(refs) - 2) * 2 * part // 1024) + 1), ff:]
    lane = lax.broadcasted_iota(jnp.int32, (count, 128), 1)
    chosen = jnp.zeros((count, 128), f32)
    for owner in range(2 * (len(refs) - 2)):
        row, shift = divmod(part * owner, 128)
        turned = pltpu.roll(lines, (128 - shift) % 128, 1)
        mine = jnp.where(lane < 128 - shift, turned[row : row + count], turned[row + 1 : row + 1 + count])
        chosen = jnp.where(lax.axis_index("dp") == owner, mine, chosen)
    vectors[...] = jnp.concatenate([chosen[i : i + 1] for i in range(count)], axis=1)[:, :part]
    for q in range(width // low):
        second[:, low * q : low * (q + 1)] = sums[high:, broad * q : broad * (q + 1)].T


def results_kernel(rows_now, outs_in, grads_in, outs_out, grads_out, pm, fetched, stage, in_sems, out_sems):
    runs = rows_now // 8
    tokens, width = outs_in.shape
    chunks = tokens // rows_now

    for source, target in ((outs_in, outs_out), (grads_in, grads_out)):

        def there(c):
            return pl.ds(pl.multiple_of(c * rows_now, rows_now), rows_now)

        def bring(c, slot):
            return pltpu.make_async_copy(source.at[there(c), :], fetched.at[slot], in_sems.at[slot])

        def send(c, slot):
            return pltpu.make_async_copy(stage.at[slot], target.at[there(c), :], out_sems.at[slot])

        bring(0, 0).start()

        def step(c):
            slot = lax.rem(c, 2)

            @pl.when(c + 1 < chunks)
            def _():
                bring(c + 1, 1 - slot).start()

            @pl.when(c >= 2)
            def _():
                send(c - 2, slot).wait()

            bring(c, slot).wait()
            for k in range(width // 128):
                cols = slice(128 * k, 128 * (k + 1))
                for m in range(rows_now // 16):
                    pair = fetched[slot, 16 * m : 16 * m + 16, cols].astype(f32)
                    for h in (0, 1):
                        pm[k, pl.ds(2 * m + h, 8, stride=runs), :] = pair[8 * h : 8 * h + 8, :]
                stage[slot, :, cols] = pm[k].astype(bf16)
            send(c, slot).start()

        loop(chunks, step)
        for c in range(max(0, chunks - 2), chunks):
            send(c, c % 2).wait()


def forward_scratch(rows, width):
    return (
        [VMEM((rows, 128), f32)]
        + [VMEM((2, rows, lane_block), f32)] * 4
        + [VMEM((rows + 24, width), f32), VMEM((rows, 128), f32)]
    )


def backward_scratch(rows, width):
    return (
        [VMEM((rows, 128), f32)]
        + [VMEM((2, rows, lane_block), f32)] * 3
        + [VMEM((rows + 24, width), f32)] * 2
        + [VMEM((rows, width), f32), VMEM((rows, 128), f32)]
    )


def params():
    return pltpu.CompilerParams(vmem_limit_bytes=vmem_mib * 2**20)


def call(kernel, plain_out, inputs, info, state, scratch, flops, name):
    kept = (pltpu.SMEM(info.shape, info.dtype),) + tuple(VMEM(s.shape, s.dtype) for s in state)
    kept_specs = [pl.BlockSpec(memory_space=pltpu.SMEM)] + [pl.BlockSpec(memory_space=VMEM) for _ in state]
    return pl.pallas_call(
        kernel,
        out_shape=tuple(plain_out) + kept,
        in_specs=[pl.BlockSpec(memory_space=VMEM) for _ in inputs] + kept_specs,
        out_specs=tuple([pl.BlockSpec(memory_space=VMEM) for _ in plain_out] + kept_specs),
        input_output_aliases={len(inputs) + i: len(plain_out) + i for i in range(len(kept))},
        scratch_shapes=scratch,
        compiler_params=params(),
        cost_estimate=pl.CostEstimate(flops=flops, bytes_accessed=0, transcendentals=0),
        name=name,
    )(*inputs, info, *state)


def body(layer_input, resets, first_weights, second_weights, section_vectors, cotangent):
    row_count, seq_length, width = layer_input.shape
    ff = first_weights.shape[2]
    hidden = ff // 2
    vector_width = section_vectors.shape[1]
    section = lax.axis_index("section")
    sections = lax.axis_size("section")
    dp_count = lax.axis_size("dp")
    tokens = row_count * seq_length
    per_row = seq_length // chunk_rows
    chunks = row_count * per_row

    keep = 1.0 - resets.astype(f32)
    keep = jnp.concatenate([jnp.zeros((row_count, 1), f32), keep[:, 1:]], axis=1).reshape(-1)

    def later(v, j):
        return jnp.concatenate([jnp.zeros((j,), f32), v[:-j]])

    def sooner(v, j):
        return jnp.concatenate([v[j:], jnp.zeros((j,), f32)])

    m1 = keep
    m2 = keep * later(keep, 1)
    m3 = m2 * later(keep, 2)
    msk = jnp.stack([m1, m2, m3, sooner(m1, 1), sooner(m2, 2), sooner(m3, 3), m1, m1], axis=1)
    msk = msk.reshape(chunks, 8, chunk_rows // 8, 8).swapaxes(1, 2).reshape(tokens, 8)


    made = (
        pltpu.SMEM((4,), jnp.int32), VMEM((tokens, columns(width, ff).end), bf16),
        VMEM((width, ff), bf16), VMEM((ff, width), bf16), VMEM((1, vector_width), f32), VMEM(msk.shape, f32),
        VMEM((8, hidden), f32), VMEM((24, width), f32), VMEM((8, hidden), f32), VMEM((24, width), f32),
        VMEM((8, vector_width), f32), VMEM((width, ff), f32), VMEM((width, ff), f32),
        VMEM((chunk_rows, width), bf16),
    )
    inputs = [
        layer_input.reshape(tokens, width), cotangent.reshape(tokens, width),
        first_weights[0], second_weights[0], section_vectors, msk,
    ]
    info, held, w1, w2, vec, msk, hs, nh, wc, gh, vacc, dw1, dw2, blank = pl.pallas_call(
        functools.partial(load_kernel, sections),
        out_shape=made,
        in_specs=[pl.BlockSpec(memory_space=pltpu.HBM)] * 6,
        out_specs=(pl.BlockSpec(memory_space=pltpu.SMEM),) + tuple(pl.BlockSpec(memory_space=VMEM) for _ in made[1:]),
        scratch_shapes=[pltpu.SemaphoreType.DMA((6,))],
        compiler_params=params(),
        name="load",
    )(
        *(pltpu.with_memory_space_constraint(v, pltpu.HBM) for v in inputs),
    )
    w1, w2, vec = (resident(v) for v in (w1, w2, vec))

    hop = hop_ticks
    base = per_row - 1 + hop * (sections - 1)
    ticks = base + chunks + hop * (sections - 1)
    plan = Plan(hop, chunks, per_row, sections)
    message = jax.ShapeDtypeStruct((chunk_rows, width), bf16)
    forward_sent, backward_sent = {}, {}
    chunk_flops = 2**10

    for t in range(ticks):
        if t < chunks + hop * (sections - 1):
            sent, info, held, msk, hs, nh = call(
                functools.partial(forward_kernel, plan),
                [message],
                [forward_sent.pop(t - hop, blank), w1, w2, vec],
                info,
                [held, msk, hs, nh],
                forward_scratch(chunk_rows, width),
                chunk_flops,
                "forward_chunk",
            )
            pairs = [(s, s + 1) for s in range(sections - 1) if 0 <= t - hop * s < chunks]
            if pairs:
                forward_sent[t] = lax.ppermute(sent, "section", pairs)
        if t >= base:
            sent, info, held, msk, vacc, wc, gh = call(
                functools.partial(backward_kernel, plan),
                [message],
                [backward_sent.pop(t - hop, blank), w1, w2, vec],
                info,
                [held, msk, vacc, wc, gh],
                backward_scratch(chunk_rows, width),
                chunk_flops,
                "backward_chunk",
            )
            pairs = [
                (s, s - 1) for s in range(1, sections) if 0 <= t - base - hop * (sections - 1 - s) < chunks
            ]
            if pairs:
                backward_sent[t] = lax.ppermute(sent, "section", pairs)
            info, held, dw1, dw2 = call(
                functools.partial(weight_kernel, plan, chunk_rows),
                [],
                [],
                info,
                [held, dw1, dw2],
                [],
                chunk_flops,
                "weight_terms",
            )
    owners = dp_count
    piece = (2 * width // owners, ff + 128)
    vmem_spec, hbm_spec = pl.BlockSpec(memory_space=VMEM), pl.BlockSpec(memory_space=pltpu.HBM)
    flat = jax.ShapeDtypeStruct((tokens, width), bf16)
    scale = (row_count * dp_count * seq_length) ** (-0.5)
    if owners == 8:
        raw_outs, raw_grads, give, own_half = pl.pallas_call(
            functools.partial(finish_kernel, owners),
            out_shape=(
                pltpu.HBM((tokens, width), bf16),
                pltpu.HBM((tokens, width), bf16),
                jax.ShapeDtypeStruct((owners // 2, *piece), bf16),
                VMEM((owners // 2, *piece), f32),
            ),
            in_specs=[vmem_spec] * 4,
            out_specs=(hbm_spec, hbm_spec, vmem_spec, vmem_spec),
            scratch_shapes=[pltpu.SemaphoreType.DMA((2,))],
            compiler_params=params(),
            name="finish",
        )(*(resident(v) for v in (held, dw1, dw2, vacc)))
        got = lax.ppermute(give, "dp", [(d, d ^ 1) for d in range(dp_count)])
        chips = dp_count // 2
        own, *sends = pl.pallas_call(
            functools.partial(share_kernel, chips),
            out_shape=(jax.ShapeDtypeStruct(piece, f32),) + (jax.ShapeDtypeStruct(piece, bf16),) * (chips - 1),
            in_specs=[vmem_spec] * 2,
            out_specs=(vmem_spec,) * chips,
            compiler_params=params(),
            name="share",
        )(resident(own_half), got)
        received = [
            lax.ppermute(sent, "dp", [(d, (d + 2 * ahead) % dp_count) for d in range(dp_count)])
            for ahead, sent in zip(range(1, chips), sends)
        ]
        first, second, vectors = pl.pallas_call(
            functools.partial(close_kernel, scale),
            out_shape=(
                jax.ShapeDtypeStruct((width // owners, ff), f32),
                jax.ShapeDtypeStruct((ff // owners, width), f32),
                jax.ShapeDtypeStruct((1, vector_width // owners), f32),
            ),
            in_specs=[vmem_spec] * chips,
            out_specs=(vmem_spec,) * 3,
            compiler_params=params(),
            name="close",
        )(own, *received)
    else:
        raw_outs, raw_grads = pl.pallas_call(
            functools.partial(raw_kernel, width, ff),
            out_shape=(pltpu.HBM((tokens, width), bf16),) * 2,
            in_specs=[vmem_spec],
            out_specs=(hbm_spec,) * 2,
            scratch_shapes=[pltpu.SemaphoreType.DMA((2,))],
            compiler_params=params(),
            name="raw",
        )(resident(held))
        first = lax.psum_scatter(dw1.astype(bf16), "dp", scatter_dimension=0, tiled=True).astype(f32) * scale
        second = lax.psum_scatter(dw2.astype(bf16), "dp", scatter_dimension=1, tiled=True).astype(f32).T * scale
        vectors = lax.psum_scatter(jnp.sum(vacc, axis=0), "dp", scatter_dimension=0, tiled=True)[None] * scale
    outs, grads = pl.pallas_call(
        functools.partial(results_kernel, chunk_rows),
        out_shape=(flat, flat),
        in_specs=[hbm_spec] * 2,
        out_specs=(hbm_spec,) * 2,
        scratch_shapes=[
            VMEM((width // 128, chunk_rows, 128), f32),
            VMEM((2, chunk_rows, width), bf16),
            VMEM((2, chunk_rows, width), bf16),
            pltpu.SemaphoreType.DMA((2,)),
            pltpu.SemaphoreType.DMA((2,)),
        ],
        compiler_params=params(),
        cost_estimate=pl.CostEstimate(flops=2**33, bytes_accessed=2**23, transcendentals=0),
        name="results",
    )(*(pltpu.with_memory_space_constraint(v, pltpu.HBM) for v in (raw_outs, raw_grads)))
    return (
        outs.reshape(1, row_count, seq_length, width),
        grads.reshape(1, row_count, seq_length, width),
        first[None],
        second[None],
        vectors,
    )


def solution(mesh):
    in_specs = (
        P("dp", None, None),
        P("dp", None),
        P("section", None, None),
        P("section", None, None),
        P("section", None),
        P("dp", None, None),
    )
    out_specs = (
        P("section", "dp", None, None),
        P("section", "dp", None, None),
        P("section", "dp", None),
        P("section", "dp", None),
        P("section", "dp"),
    )
    return jax.shard_map(body, mesh=mesh, in_specs=in_specs, out_specs=out_specs, check_vma=False)
```

```python
import functools
import typing

import jax
import jax.numpy as jnp
from jax import lax
from jax.experimental import pallas as pl
from jax.experimental.pallas import tpu as pltpu
from jax.sharding import PartitionSpec as P

norm_eps = 1e-05
chunk_rows = 256
hop_ticks = 2
lane_block = 256
tall = 64
half_rows = 128
vmem_mib = 6
f32 = jnp.float32
bf16 = jnp.bfloat16
VMEM = pltpu.VMEM


def resident(array):
    return pltpu.with_memory_space_constraint(array, VMEM)


def nn(left, right):
    return jnp.dot(left, right, preferred_element_type=f32)


def tn(left, right):
    return lax.dot_general(left, right, (((0,), (0,)), ((), ())), preferred_element_type=f32)


def nt(left, right):
    return lax.dot_general(left, right, (((1,), (1,)), ((), ())), preferred_element_type=f32)


def logistic(v):
    return pl.reciprocal(1.0 + jnp.exp(-v), approx=True)


def by_eight(v):
    return jnp.sum(v.reshape(v.shape[0] // 8, 8, v.shape[1]), axis=0)


def span(base, step, size):
    if isinstance(base, int) and isinstance(step, int):
        return slice(base + step, base + step + size)
    return pl.ds(pl.multiple_of(base + step, 128), size)


def lines(first, size, multiple=8):
    if isinstance(first, int):
        return slice(first, first + size)
    return pl.ds(pl.multiple_of(first, multiple), size)


def doubled(v, axis=0):
    return jnp.concatenate([v, v], axis=axis)


def place_of(shape):
    return lax.broadcasted_iota(jnp.int32, shape, 0)


def across(run, prod, carry, backward):
    place = place_of(run.shape)
    for d in (1, 2, 4):
        seen = place < 8 - d if backward else place >= d
        shift = 8 - d if backward else d
        prod_before = jnp.where(seen, pltpu.roll(prod, shift, 0), 1.0)
        run_before = jnp.where(seen, pltpu.roll(run, shift, 0), 0.0)
        run = run + prod * run_before
        prod = prod * prod_before
    ends = run + prod * carry
    if backward:
        return jnp.where(place < 7, pltpu.roll(ends, 7, 0), carry), ends[0:1, :]
    return jnp.where(place >= 1, pltpu.roll(ends, 1, 0), carry), ends[7:8, :]


def norm_factor(x):
    return lax.rsqrt(jnp.mean(x * x, axis=-1, keepdims=True) + norm_eps)


class Columns(typing.NamedTuple):
    stream: int
    normed: int
    left: int
    grad: int
    outs: int
    sent: int
    wide_a: int
    wide_b: int
    slope: int
    end: int


def columns(width, ff):
    wide = 6 * width + 2 * ff
    return Columns(*(width * i for i in range(7)), 6 * width + ff, wide, wide + ff // 2)


class Plan(typing.NamedTuple):
    hop: int
    chunks: int
    per_row: int
    sections: int


def forward_turn(plan, info):
    c = info[2] - plan.hop * info[0]
    return jnp.clip(c, 0, plan.chunks - 1), (c >= 0) & (c < plan.chunks)


def backward_turn(plan, info):
    j = info[3] - plan.hop * (plan.sections - 1 - info[0])
    return jnp.clip(j, 0, plan.chunks - 1), (j >= 0) & (j < plan.chunks)


def backward_chunk(plan, j):
    behind = lax.rem(j, plan.per_row)
    return j - behind + plan.per_row - 1 - behind


def loop(count, step):
    lax.fori_loop(0, count, lambda i, carry: (step(i), carry)[1], 0)


def unrolled(count, step):
    for b in range(count):
        step(b)


def into_runs(held, start, rows_now, column, width, p_s):
    runs = rows_now // 8

    def step(k):
        cols = span(column, 128 * k, 128)
        p_s[:, 0:128] = held[pl.ds(start, rows_now), cols].astype(f32)
        for m in range(rows_now // 16):
            pair = [p_s[pl.ds(2 * m + h, 8, stride=runs), :] for h in (0, 1)]
            held[pl.ds(pl.multiple_of(start + 16 * m, 16), 16), cols] = jnp.concatenate(pair, axis=0).astype(bf16)

    loop(width // 128, step)


def forward_kernel(
    plan, recv, w1, w2, vec,
    sc_in, held_in, msk_in, hs_in, nh_in, send, sc, held, msk, hs, nh,
    pm, p_2, q_2, e_2, g_2, nx, kp,
):
    rows_now, width = recv.shape
    ff = w1.shape[1]
    hidden = ff // 2
    col = columns(width, ff)
    c, active = forward_turn(plan, sc)
    start = pl.multiple_of(c * rows_now, rows_now)
    rows = pl.ds(start, rows_now)
    mixer = sc[1] == 0
    tail = width + ff
    tiles = rows_now // 16
    narrow = lambda base: slice(base, base + width)

    def at(r, size):
        return pl.ds(pl.multiple_of(start + r, 16), size)

    @pl.when(active & (sc[0] > 0))
    def _():
        held[rows, narrow(col.stream)] = recv[...]

    @pl.when(active & (sc[0] == 0))
    def _():
        into_runs(held, start, rows_now, col.stream, width, pm)

    @pl.when(active & mixer)
    def _():
        gain = vec[:, :width]

        def norm_step(i):
            here = at(tall * i, tall)
            x = held[here, narrow(col.stream)].astype(f32)
            factor = norm_factor(x)
            normed = x * factor * gain
            nx[lines(24 + tall * i, tall, 8), :] = normed
            held[here, narrow(col.normed)] = normed.astype(bf16)
            msk[here, 6:7] = factor
            kp[lines(tall * i, tall, 8), :] = jnp.broadcast_to(msk[here, 0:1], (tall, 128))

        unrolled(rows_now // tall, norm_step)
        place = place_of((8, width))
        for g in range(0, 24, 8):
            rolled = pltpu.roll(nx[rows_now + g : rows_now + g + 8, :], 1, 0)
            nx[g : g + 8, :] = jnp.where(place == 0, nh[g : g + 8, :], rolled)
            nh[g : g + 8, :] = rolled

        def conv_step(i):
            here = at(tall * i, tall)
            conv = nx[lines(24 + tall * i, tall, 8), :] * vec[:, width : 2 * width]
            for j in range(1, ff // width):
                tap = vec[:, (1 + j) * width : (2 + j) * width]
                earlier = nx[lines(24 - 8 * j + tall * i, tall, 8), :]
                conv = conv + earlier * (msk[here, j - 1 : j] * tap)
            held[here, narrow(col.left)] = conv.astype(bf16)

        unrolled(rows_now // tall, conv_step)

        def hidden_step(b):
            own = span(0, lane_block * b, lane_block)
            conv16 = held[rows, narrow(col.left)]
            p_s, q_s, e_s, g_s = (ref.at[b % 2] for ref in (p_2, q_2, e_2, g_2))
            p_s[...] = nn(conv16, w1[:, own])
            e_s[...] = nn(conv16, w1[:, span(hidden, lane_block * b, lane_block)])
            g_s[...] = nt(held[rows, narrow(col.normed)], w2[span(hidden, lane_block * b, lane_block), :])
            bias = vec[:, span(tail, lane_block * b, lane_block)]
            on = lambda base: span(base, lane_block * b, lane_block)
            run = prod = None
            for m in range(tiles):
                r = 16 * m
                update = logistic(p_s[r : r + 16, :] + bias)
                held[at(r, 16), on(col.wide_a)] = update.astype(bf16)
                decay = (1.0 - update) * doubled(kp[r : r + 16, :], 1)
                fresh = update * e_s[r : r + 16, :]
                for h in (0, 8):
                    a, v = decay[h : h + 8, :], fresh[h : h + 8, :]
                    run, prod = (v, a) if run is None else (a * run + v, prod * a)
                    p_s[r + h : r + h + 8, :] = prod
                    q_s[r + h : r + h + 8, :] = run
            inward, last = across(run, prod, hs[0:1, own], False)
            hs[0:1, own] = last
            inward = doubled(inward)
            for m in range(tiles):
                r = 16 * m
                states = q_s[r : r + 16, :] + p_s[r : r + 16, :] * inward
                gate = g_s[r : r + 16, :]
                sig = logistic(gate)
                act = gate * sig
                held[at(r, 16), on(col.wide_b)] = (states * act).astype(bf16)
                held[at(r, 16), on(col.slope)] = act.astype(bf16)
                held[at(r, 16), on(col.wide_b + hidden)] = (states * (sig + act * (1.0 - sig))).astype(bf16)
                update = held[at(r, 16), on(col.wide_a)].astype(f32)
                held[at(r, 16), on(col.wide_a + hidden)] = (update * (e_s[r : r + 16, :] - states)).astype(bf16)

        unrolled(hidden // lane_block, hidden_step)

        def out_step(b):
            own = span(0, lane_block * b, lane_block)
            x = held[rows, span(col.stream, lane_block * b, lane_block)].astype(f32)
            result = (x + nn(held[rows, col.wide_b : col.wide_b + hidden], w2[:hidden, own])).astype(bf16)
            send[:, own] = result
            held[rows, span(col.outs, lane_block * b, lane_block)] = result

        unrolled(width // lane_block, out_step)

    @pl.when(active & jnp.logical_not(mixer))
    def _():
        gain = vec[:, :width]

        def norm_step(i):
            here = at(tall * i, tall)
            x = held[here, narrow(col.stream)].astype(f32)
            factor = norm_factor(x)
            msk[here, 6:7] = factor
            held[here, narrow(col.left)] = (x * factor * gain).astype(bf16)

        unrolled(rows_now // tall, norm_step)

        def half_step(i):
            here = at(half_rows * i, half_rows)
            norm16 = held[here, narrow(col.left)]
            for lo in range(0, ff, lane_block):
                hi = lo + lane_block
                h = nn(norm16, w1[:, lo:hi]) + vec[:, width + lo : width + hi]
                square = h * h
                bend = jnp.tanh(h * (0.7978845608 + (0.7978845608 * 0.044715) * square))
                half = 0.5 + 0.5 * bend
                held[here, col.wide_b + lo : col.wide_b + hi] = (h * half).astype(bf16)
                slope = half + (h * (1.0 - bend * bend)) * (
                    0.5 * 0.7978845608 + (0.5 * 0.7978845608 * 3.0 * 0.044715) * square
                )
                held[here, col.wide_a + lo : col.wide_a + hi] = slope.astype(bf16)
            down = nn(held[here, col.wide_b : col.slope], w2[...])
            held[here, narrow(col.normed)] = down.astype(bf16)
            x = held[here, narrow(col.stream)].astype(f32)
            result = (x + (down * vec[:, tail : tail + width] + vec[:, tail + width : tail + 2 * width])).astype(bf16)
            send[lines(half_rows * i, half_rows, 16), :] = result
            held[here, narrow(col.outs)] = result

        loop(rows_now // half_rows, half_step)

    sc[2] = sc[2] + 1


def norm_backward(x, factor, gain, grad_normed, grads_wide, vacc):
    width = x.shape[1]
    scaled = x * factor
    vacc[:, :width] = vacc[:, :width] + by_eight(grad_normed * scaled)
    e = grad_normed * gain
    level = jnp.mean(e * scaled, axis=-1, keepdims=True)
    return (grads_wide + factor * (e - scaled * level)).astype(bf16)


def backward_kernel(
    plan, recv, w1, w2, vec,
    sc_in, held_in, msk_in, vacc_in, wc_in, gh_in, send, sc, held, msk, vacc, wc, gh,
    pm, p_2, q_2, g_2, nx, gx, gn, kp,
):
    rows_now, width = recv.shape
    ff = w1.shape[1]
    hidden = ff // 2
    col = columns(width, ff)
    j, active = backward_turn(plan, sc)
    start = pl.multiple_of(backward_chunk(plan, j) * rows_now, rows_now)
    rows = pl.ds(start, rows_now)
    mixer = sc[1] == 0
    tail = width + ff
    tiles = rows_now // 16
    narrow = lambda base: slice(base, base + width)

    def at(r, size):
        return pl.ds(pl.multiple_of(start + r, 16), size)

    def before(size):
        return pl.ds(pl.multiple_of(jnp.maximum(start - size, 0), 16), size)

    @pl.when(active & (sc[0] < plan.sections - 1))
    def _():
        held[rows, narrow(col.grad)] = recv[...]

    @pl.when(active & (sc[0] == plan.sections - 1))
    def _():
        into_runs(held, start, rows_now, col.grad, width, pm)

    def add(cols, value):
        vacc[:, cols] = vacc[:, cols] + value

    @pl.when(active & mixer)
    def _():
        gain = vec[:, :width]

        def norm_step(i):
            here = at(tall * i, tall)
            nx[lines(24 + tall * i, tall, 8), :] = held[here, narrow(col.normed)].astype(f32)
            kp[lines(tall * i, tall, 8), :] = jnp.broadcast_to(msk[here, 0:1], (tall, 128))

        unrolled(rows_now // tall, norm_step)
        n_before = held[before(32), narrow(col.normed)].astype(f32)[8:32, :]
        place = place_of((8, width))
        for g in range(0, 24, 8):
            nx[g : g + 8, :] = pltpu.roll(
                jnp.where(place == 7, n_before[g : g + 8, :], nx[rows_now + g : rows_now + g + 8, :]), 1, 0
            )

        def hidden_step(b):
            own = span(0, lane_block * b, lane_block)
            on = lambda base: span(base, lane_block * b, lane_block)
            p_s, q_s, g_s = (ref.at[0] for ref in (p_2, q_2, g_2))
            g_s[...] = nt(held[rows, narrow(col.grad)], w2[own, :])
            run = prod = None
            for m in range(tiles - 1, -1, -1):
                r = 16 * m
                grad_merged = g_s[r : r + 16, :]
                turn = held[at(r, 16), on(col.wide_b + hidden)].astype(f32)
                held[at(r, 16), on(col.wide_b + hidden)] = (grad_merged * turn).astype(bf16)
                update = held[at(r, 16), on(col.wide_a)].astype(f32)
                decay = (1.0 - update) * doubled(kp[r : r + 16, :], 1)
                grad_states = grad_merged * held[at(r, 16), on(col.slope)].astype(f32)
                for h in (8, 0):
                    a, v = decay[h : h + 8, :], grad_states[h : h + 8, :]
                    if run is None:
                        prod = jnp.ones_like(v)
                    else:
                        v = v + run
                    q_s[r + h : r + h + 8, :] = v
                    p_s[r + h : r + h + 8, :] = prod
                    run, prod = a * v, prod * a
            inward, last = across(run, prod, wc[0:1, own], True)
            wc[0:1, own] = last
            inward = doubled(inward)
            total = jnp.zeros((8, lane_block), f32)
            for m in range(tiles):
                r = 16 * m
                carried = q_s[r : r + 16, :] + p_s[r : r + 16, :] * inward
                update = held[at(r, 16), on(col.wide_a)].astype(f32)
                up16 = (carried * held[at(r, 16), on(col.wide_a + hidden)].astype(f32)).astype(bf16)
                held[at(r, 16), on(col.wide_a)] = up16
                held[at(r, 16), on(col.wide_a + hidden)] = (carried * update).astype(bf16)
                up = up16.astype(f32)
                total = total + (up[0:8, :] + up[8:16, :])
            add(on(tail), total)

        loop(hidden // lane_block, hidden_step)

        def product_step(b):
            own = span(0, lane_block * b, lane_block)
            gx[0:rows_now, own] = nt(held[rows, col.wide_a : col.wide_b], w1[own, :])
            gn[:, own] = nn(held[rows, col.wide_b + hidden : col.slope], w2[hidden:, own])

        unrolled(width // lane_block, product_step)
        for g in range(0, 24, 8):
            rolled = pltpu.roll(gx[g : g + 8, :], 7, 0)
            gx[rows_now + g : rows_now + g + 8, :] = jnp.where(place == 7, gh[g : g + 8, :], rolled)
            gh[g : g + 8, :] = rolled

        def out_step(i):
            here = at(tall * i, tall)
            x = held[here, narrow(col.stream)].astype(f32)
            factor = msk[here, 6:7]
            base = tall * i
            grad_conv = gx[lines(base, tall, 8), :]
            grad_normed = gn[lines(base, tall, 8), :] + vec[:, width : 2 * width] * grad_conv
            add(slice(width, 2 * width), by_eight(grad_conv * nx[lines(24 + base, tall, 8), :]))
            for k in range(1, ff // width):
                cols = slice((1 + k) * width, (2 + k) * width)
                ahead = gx[lines(base + 8 * k, tall, 8), :]
                grad_normed = grad_normed + ahead * (vec[:, cols] * msk[here, 2 + k : 3 + k])
                earlier = nx[lines(24 - 8 * k + base, tall, 8), :]
                add(cols, by_eight(grad_conv * (earlier * msk[here, k - 1 : k])))
            grads_wide = held[here, narrow(col.grad)].astype(f32)
            result = norm_backward(x, factor, gain, grad_normed, grads_wide, vacc)
            send[lines(base, tall, 16), :] = result
            held[here, narrow(col.sent)] = result

        unrolled(rows_now // tall, out_step)

    @pl.when(active & jnp.logical_not(mixer))
    def _():
        gain = vec[:, :width]

        def scale_step(i):
            here = at(tall * i, tall)
            grads_wide = held[here, narrow(col.grad)].astype(f32)
            down = held[here, narrow(col.normed)].astype(f32)
            add(slice(tail, tail + width), by_eight(grads_wide * down))
            add(slice(tail + width, tail + 2 * width), by_eight(grads_wide))
            held[here, narrow(col.normed)] = (grads_wide * vec[:, tail : tail + width]).astype(bf16)

        unrolled(rows_now // tall, scale_step)

        def hidden_step(b):
            for u in range(1):
                at_b = 1 * lane_block * b + u * lane_block
                on = lambda base: span(base, at_b, lane_block)
                grad_active = nt(held[rows, narrow(col.normed)], w2[on(0), :])
                hid16 = (grad_active * held[rows, on(col.wide_a)].astype(f32)).astype(bf16)
                held[rows, on(col.wide_a)] = hid16
                add(on(width), by_eight(hid16.astype(f32)))

        unrolled(ff // (lane_block * 1), hidden_step)

        def product_step(b):
            own = span(0, lane_block * b, lane_block)
            gn[:, own] = nt(held[rows, col.wide_a : col.wide_b], w1[own, :])

        unrolled(width // lane_block, product_step)

        def out_step(i):
            here = at(tall * i, tall)
            x = held[here, narrow(col.stream)].astype(f32)
            grads_wide = held[here, narrow(col.grad)].astype(f32)
            grad_normed = gn[lines(tall * i, tall, 8), :]
            result = norm_backward(x, msk[here, 6:7], gain, grad_normed, grads_wide, vacc)
            send[lines(tall * i, tall, 16), :] = result
            held[here, narrow(col.sent)] = result

        unrolled(rows_now // tall, out_step)


def weight_kernel(
    plan, rows_now, sc_in, held_in, dw1_in, dw2_in, sc, held, dw1, dw2,
):
    width, ff = dw1.shape
    hidden = ff // 2
    col = columns(width, ff)
    late = sc[0] >= plan.sections // 2
    j = sc[3] - plan.hop * (plan.sections - 1)
    waited = plan.chunks // 2
    first = jnp.where(late, 2 * (j - waited), j)
    count = jnp.where(first < 0, 0, jnp.where(late, 2, 1))

    @pl.when((sc[0] == 0) & (j == -1))
    def _():
        dw1[...] = jnp.zeros_like(dw1)
        dw2[...] = jnp.zeros_like(dw2)

    def unit(i):
        rows = pl.ds(pl.multiple_of(backward_chunk(plan, first + i) * rows_now, rows_now), rows_now)

        def terms(ref, left, right, size, into):
            block = 512
            for lo in range(0, size, block):
                term = tn(left, held[rows, right + lo : right + lo + block])
                cols = slice(into + lo, into + lo + block)
                ref[:, cols] = ref[:, cols] + term

        terms(dw1, held[rows, col.left : col.left + width], col.wide_a, ff, 0)
        upper = jnp.where(sc[1] == 0, col.grad, col.normed)
        terms(dw2, held[rows, span(upper, 0, width)], col.wide_b, hidden, 0)
        terms(dw2, held[rows, col.normed : col.normed + width], col.wide_b + hidden, hidden, hidden)

    loop(count, unit)

    sc[3] = sc[3] + 1


def load_kernel(sections, x_hbm, g_hbm, w1_hbm, w2_hbm, vec_hbm, msk_hbm,
                info, held, w1, w2, vec, msk, hs, nh, wc, gh, vacc, dw1, dw2, blank, sems):
    width, ff = w1.shape
    col = columns(width, ff)
    section = lax.axis_index("section")
    info[0] = section
    info[1] = lax.rem(section, 2)
    info[2] = 0
    info[3] = 0
    moves = [(w1_hbm, w1), (w2_hbm, w2), (vec_hbm, vec), (msk_hbm, msk)]
    copies = [pltpu.make_async_copy(a, b, sems.at[i]) for i, (a, b) in enumerate(moves)]
    first = pltpu.make_async_copy(x_hbm, held.at[:, col.stream : col.stream + width], sems.at[4])
    last = pltpu.make_async_copy(g_hbm, held.at[:, col.grad : col.grad + width], sems.at[5])
    for copy in copies:
        copy.start()

    @pl.when(section == 0)
    def _():
        first.start()

    @pl.when(section == sections - 1)
    def _():
        last.start()

    for ref in (hs, nh, wc, gh, vacc, blank):
        ref[...] = jnp.zeros_like(ref)

    @pl.when(section > 0)
    def _():
        dw1[...] = jnp.zeros_like(dw1)
        dw2[...] = jnp.zeros_like(dw2)

    for copy in copies:
        copy.wait()

    @pl.when(section == 0)
    def _():
        first.wait()

    @pl.when(section == sections - 1)
    def _():
        last.wait()


def piece_of(dw1, dw2, owner, owners):
    width, ff = dw1.shape
    high, broad = width // owners, ff // owners
    count = ff // broad
    low = width // count
    yield 0, high, dw1[pl.ds(pl.multiple_of(high * owner, 8), high), :]
    cols = span(0, broad * owner, broad)
    parts = [dw2[low * q : low * (q + 1), cols] for q in range(count)]
    yield high, low, jnp.concatenate(parts, axis=1)


def finish_kernel(owners, held, dw1, dw2, vacc, outs_out, grads_out, give, keep, sems):
    width, ff = dw1.shape
    col = columns(width, ff)
    copies = [
        pltpu.make_async_copy(held.at[:, base : base + width], target, sems.at[i])
        for i, (base, target) in enumerate(((col.outs, outs_out), (col.sent, grads_out)))
    ]
    for copy in copies:
        copy.start()
    core = lax.rem(lax.axis_index("dp"), 2)
    line = jnp.sum(vacc[...], axis=0, keepdims=True)
    lines = line.shape[1] // 128
    total = jnp.concatenate(
        [line[:, 128 * i : 128 * (i + 1)] for i in range(lines)]
        + [jnp.zeros((give.shape[1] - lines, 128), f32)],
        axis=0,
    )

    def step(z):
        for mine, ref in ((core, keep), (1 - core, give)):
            for at, size, value in piece_of(dw1, dw2, 2 * z + mine, owners):
                ref[z, at : at + size, 0:ff] = value.astype(ref.dtype)
            ref[z, :, ff:] = total.astype(ref.dtype)

    loop(owners // 2, step)
    for copy in copies:
        copy.wait()


def raw_kernel(width, ff, held, outs_out, grads_out, sems):
    col = columns(width, ff)
    copies = [
        pltpu.make_async_copy(held.at[:, base : base + width], target, sems.at[i])
        for i, (base, target) in enumerate(((col.outs, outs_out), (col.sent, grads_out)))
    ]
    for copy in copies:
        copy.start()
    for copy in copies:
        copy.wait()


def share_kernel(chips, keep, got, own, *sends):
    chip = lax.div(lax.axis_index("dp"), 2)
    for ahead, ref in enumerate((own, *sends)):
        z = lax.rem(chip + ahead, chips)
        ref[...] = (keep[z] + got[z].astype(f32)).astype(ref.dtype)


def close_kernel(scale, own, *refs):
    received, (first, second, vectors) = refs[:-3], refs[-3:]
    high = first.shape[0]
    sums = own[...]
    for ref in received:
        sums = sums + ref[...].astype(f32)
    sums = sums * scale
    broad, width = second.shape
    low = sums.shape[0] - high
    ff = first.shape[1]
    first[...] = sums[0:high, 0:ff]
    part = vectors.shape[1]
    count = -(-part // 128)
    lines = sums[0 : 8 * (-(-(len(refs) - 2) * 2 * part // 1024) + 1), ff:]
    lane = lax.broadcasted_iota(jnp.int32, (count, 128), 1)
    chosen = jnp.zeros((count, 128), f32)
    for owner in range(2 * (len(refs) - 2)):
        row, shift = divmod(part * owner, 128)
        turned = pltpu.roll(lines, (128 - shift) % 128, 1)
        mine = jnp.where(lane < 128 - shift, turned[row : row + count], turned[row + 1 : row + 1 + count])
        chosen = jnp.where(lax.axis_index("dp") == owner, mine, chosen)
    vectors[...] = jnp.concatenate([chosen[i : i + 1] for i in range(count)], axis=1)[:, :part]
    for q in range(width // low):
        second[:, low * q : low * (q + 1)] = sums[high:, broad * q : broad * (q + 1)].T


def results_kernel(rows_now, outs_in, grads_in, outs_out, grads_out, pm, fetched, stage, in_sems, out_sems):
    runs = rows_now // 8
    tokens, width = outs_in.shape
    chunks = tokens // rows_now

    for source, target in ((outs_in, outs_out), (grads_in, grads_out)):

        def there(c):
            return pl.ds(pl.multiple_of(c * rows_now, rows_now), rows_now)

        def bring(c, slot):
            return pltpu.make_async_copy(source.at[there(c), :], fetched.at[slot], in_sems.at[slot])

        def send(c, slot):
            return pltpu.make_async_copy(stage.at[slot], target.at[there(c), :], out_sems.at[slot])

        bring(0, 0).start()

        def step(c):
            slot = lax.rem(c, 2)

            @pl.when(c + 1 < chunks)
            def _():
                bring(c + 1, 1 - slot).start()

            @pl.when(c >= 2)
            def _():
                send(c - 2, slot).wait()

            bring(c, slot).wait()
            for k in range(width // 128):
                cols = slice(128 * k, 128 * (k + 1))
                for m in range(rows_now // 16):
                    pair = fetched[slot, 16 * m : 16 * m + 16, cols].astype(f32)
                    for h in (0, 1):
                        pm[k, pl.ds(2 * m + h, 8, stride=runs), :] = pair[8 * h : 8 * h + 8, :]
                stage[slot, :, cols] = pm[k].astype(bf16)
            send(c, slot).start()

        loop(chunks, step)
        for c in range(max(0, chunks - 2), chunks):
            send(c, c % 2).wait()


def forward_scratch(rows, width):
    return (
        [VMEM((rows, 128), f32)]
        + [VMEM((2, rows, lane_block), f32)] * 4
        + [VMEM((rows + 24, width), f32), VMEM((rows, 128), f32)]
    )


def backward_scratch(rows, width):
    return (
        [VMEM((rows, 128), f32)]
        + [VMEM((2, rows, lane_block), f32)] * 3
        + [VMEM((rows + 24, width), f32)] * 2
        + [VMEM((rows, width), f32), VMEM((rows, 128), f32)]
    )


def params():
    return pltpu.CompilerParams(vmem_limit_bytes=vmem_mib * 2**20)


def call(kernel, plain_out, inputs, info, state, scratch, flops, name):
    kept = (pltpu.SMEM(info.shape, info.dtype),) + tuple(VMEM(s.shape, s.dtype) for s in state)
    kept_specs = [pl.BlockSpec(memory_space=pltpu.SMEM)] + [pl.BlockSpec(memory_space=VMEM) for _ in state]
    return pl.pallas_call(
        kernel,
        out_shape=tuple(plain_out) + kept,
        in_specs=[pl.BlockSpec(memory_space=VMEM) for _ in inputs] + kept_specs,
        out_specs=tuple([pl.BlockSpec(memory_space=VMEM) for _ in plain_out] + kept_specs),
        input_output_aliases={len(inputs) + i: len(plain_out) + i for i in range(len(kept))},
        scratch_shapes=scratch,
        compiler_params=params(),
        cost_estimate=pl.CostEstimate(flops=flops, bytes_accessed=0, transcendentals=0),
        name=name,
    )(*inputs, info, *state)


def body(layer_input, resets, first_weights, second_weights, section_vectors, cotangent):
    row_count, seq_length, width = layer_input.shape
    ff = first_weights.shape[2]
    hidden = ff // 2
    vector_width = section_vectors.shape[1]
    section = lax.axis_index("section")
    sections = lax.axis_size("section")
    dp_count = lax.axis_size("dp")
    tokens = row_count * seq_length
    per_row = seq_length // chunk_rows
    chunks = row_count * per_row

    keep = 1.0 - resets.astype(f32)
    keep = jnp.concatenate([jnp.zeros((row_count, 1), f32), keep[:, 1:]], axis=1).reshape(-1)

    def later(v, j):
        return jnp.concatenate([jnp.zeros((j,), f32), v[:-j]])

    def sooner(v, j):
        return jnp.concatenate([v[j:], jnp.zeros((j,), f32)])

    m1 = keep
    m2 = keep * later(keep, 1)
    m3 = m2 * later(keep, 2)
    msk = jnp.stack([m1, m2, m3, sooner(m1, 1), sooner(m2, 2), sooner(m3, 3), m1, m1], axis=1)
    msk = msk.reshape(chunks, 8, chunk_rows // 8, 8).swapaxes(1, 2).reshape(tokens, 8)


    made = (
        pltpu.SMEM((4,), jnp.int32), VMEM((tokens, columns(width, ff).end), bf16),
        VMEM((width, ff), bf16), VMEM((ff, width), bf16), VMEM((1, vector_width), f32), VMEM(msk.shape, f32),
        VMEM((8, hidden), f32), VMEM((24, width), f32), VMEM((8, hidden), f32), VMEM((24, width), f32),
        VMEM((8, vector_width), f32), VMEM((width, ff), f32), VMEM((width, ff), f32),
        VMEM((chunk_rows, width), bf16),
    )
    inputs = [
        layer_input.reshape(tokens, width), cotangent.reshape(tokens, width),
        first_weights[0], second_weights[0], section_vectors, msk,
    ]
    info, held, w1, w2, vec, msk, hs, nh, wc, gh, vacc, dw1, dw2, blank = pl.pallas_call(
        functools.partial(load_kernel, sections),
        out_shape=made,
        in_specs=[pl.BlockSpec(memory_space=pltpu.HBM)] * 6,
        out_specs=(pl.BlockSpec(memory_space=pltpu.SMEM),) + tuple(pl.BlockSpec(memory_space=VMEM) for _ in made[1:]),
        scratch_shapes=[pltpu.SemaphoreType.DMA((6,))],
        compiler_params=params(),
        name="load",
    )(
        *(pltpu.with_memory_space_constraint(v, pltpu.HBM) for v in inputs),
    )
    w1, w2, vec = (resident(v) for v in (w1, w2, vec))

    hop = hop_ticks
    base = per_row - 1 + hop * (sections - 1)
    ticks = base + chunks + hop * (sections - 1)
    plan = Plan(hop, chunks, per_row, sections)
    message = jax.ShapeDtypeStruct((chunk_rows, width), bf16)
    forward_sent, backward_sent = {}, {}
    chunk_flops = 2**10

    for t in range(ticks):
        if t < chunks + hop * (sections - 1):
            sent, info, held, msk, hs, nh = call(
                functools.partial(forward_kernel, plan),
                [message],
                [forward_sent.pop(t - hop, blank), w1, w2, vec],
                info,
                [held, msk, hs, nh],
                forward_scratch(chunk_rows, width),
                chunk_flops,
                "forward_chunk",
            )
            pairs = [(s, s + 1) for s in range(sections - 1) if 0 <= t - hop * s < chunks]
            if pairs:
                forward_sent[t] = lax.ppermute(sent, "section", pairs)
        if t >= base:
            sent, info, held, msk, vacc, wc, gh = call(
                functools.partial(backward_kernel, plan),
                [message],
                [backward_sent.pop(t - hop, blank), w1, w2, vec],
                info,
                [held, msk, vacc, wc, gh],
                backward_scratch(chunk_rows, width),
                chunk_flops,
                "backward_chunk",
            )
            pairs = [
                (s, s - 1) for s in range(1, sections) if 0 <= t - base - hop * (sections - 1 - s) < chunks
            ]
            if pairs:
                backward_sent[t] = lax.ppermute(sent, "section", pairs)
            info, held, dw1, dw2 = call(
                functools.partial(weight_kernel, plan, chunk_rows),
                [],
                [],
                info,
                [held, dw1, dw2],
                [],
                chunk_flops,
                "weight_terms",
            )
    owners = dp_count
    piece = (2 * width // owners, ff + 128)
    vmem_spec, hbm_spec = pl.BlockSpec(memory_space=VMEM), pl.BlockSpec(memory_space=pltpu.HBM)
    flat = jax.ShapeDtypeStruct((tokens, width), bf16)
    scale = (row_count * dp_count * seq_length) ** (-0.5)
    if owners == 8:
        raw_outs, raw_grads, give, own_half = pl.pallas_call(
            functools.partial(finish_kernel, owners),
            out_shape=(
                pltpu.HBM((tokens, width), bf16),
                pltpu.HBM((tokens, width), bf16),
                jax.ShapeDtypeStruct((owners // 2, *piece), bf16),
                VMEM((owners // 2, *piece), f32),
            ),
            in_specs=[vmem_spec] * 4,
            out_specs=(hbm_spec, hbm_spec, vmem_spec, vmem_spec),
            scratch_shapes=[pltpu.SemaphoreType.DMA((2,))],
            compiler_params=params(),
            name="finish",
        )(*(resident(v) for v in (held, dw1, dw2, vacc)))
        got = lax.ppermute(give, "dp", [(d, d ^ 1) for d in range(dp_count)])
        chips = dp_count // 2
        own, *sends = pl.pallas_call(
            functools.partial(share_kernel, chips),
            out_shape=(jax.ShapeDtypeStruct(piece, f32),) + (jax.ShapeDtypeStruct(piece, bf16),) * (chips - 1),
            in_specs=[vmem_spec] * 2,
            out_specs=(vmem_spec,) * chips,
            compiler_params=params(),
            name="share",
        )(resident(own_half), got)
        received = [
            lax.ppermute(sent, "dp", [(d, (d + 2 * ahead) % dp_count) for d in range(dp_count)])
            for ahead, sent in zip(range(1, chips), sends)
        ]
        first, second, vectors = pl.pallas_call(
            functools.partial(close_kernel, scale),
            out_shape=(
                jax.ShapeDtypeStruct((width // owners, ff), f32),
                jax.ShapeDtypeStruct((ff // owners, width), f32),
                jax.ShapeDtypeStruct((1, vector_width // owners), f32),
            ),
            in_specs=[vmem_spec] * chips,
            out_specs=(vmem_spec,) * 3,
            compiler_params=params(),
            name="close",
        )(own, *received)
    else:
        raw_outs, raw_grads = pl.pallas_call(
            functools.partial(raw_kernel, width, ff),
            out_shape=(pltpu.HBM((tokens, width), bf16),) * 2,
            in_specs=[vmem_spec],
            out_specs=(hbm_spec,) * 2,
            scratch_shapes=[pltpu.SemaphoreType.DMA((2,))],
            compiler_params=params(),
            name="raw",
        )(resident(held))
        first = lax.psum_scatter(dw1.astype(bf16), "dp", scatter_dimension=0, tiled=True).astype(f32) * scale
        second = lax.psum_scatter(dw2.astype(bf16), "dp", scatter_dimension=1, tiled=True).astype(f32).T * scale
        vectors = lax.psum_scatter(jnp.sum(vacc, axis=0), "dp", scatter_dimension=0, tiled=True)[None] * scale
    outs, grads = pl.pallas_call(
        functools.partial(results_kernel, chunk_rows),
        out_shape=(flat, flat),
        in_specs=[hbm_spec] * 2,
        out_specs=(hbm_spec,) * 2,
        scratch_shapes=[
            VMEM((width // 128, chunk_rows, 128), f32),
            VMEM((2, chunk_rows, width), bf16),
            VMEM((2, chunk_rows, width), bf16),
            pltpu.SemaphoreType.DMA((2,)),
            pltpu.SemaphoreType.DMA((2,)),
        ],
        compiler_params=params(),
        cost_estimate=pl.CostEstimate(flops=2**33, bytes_accessed=2**23, transcendentals=0),
        name="results",
    )(*(pltpu.with_memory_space_constraint(v, pltpu.HBM) for v in (raw_outs, raw_grads)))
    return (
        outs.reshape(1, row_count, seq_length, width),
        grads.reshape(1, row_count, seq_length, width),
        first[None],
        second[None],
        vectors,
    )


def solution(mesh):
    in_specs = (
        P("dp", None, None),
        P("dp", None),
        P("section", None, None),
        P("section", None, None),
        P("section", None),
        P("dp", None, None),
    )
    out_specs = (
        P("section", "dp", None, None),
        P("section", "dp", None, None),
        P("section", "dp", None),
        P("section", "dp", None),
        P("section", "dp"),
    )
    return jax.shard_map(body, mesh=mesh, in_specs=in_specs, out_specs=out_specs, check_vma=False)
```

```python
import functools
import typing

import jax
import jax.numpy as jnp
from jax import lax
from jax.experimental import pallas as pl
from jax.experimental.pallas import tpu as pltpu
from jax.sharding import PartitionSpec as P

norm_eps = 1e-05
chunk_rows = 256
hop_ticks = 2
lane_block = 256
tall = 128
vmem_mib = 6
f32 = jnp.float32
bf16 = jnp.bfloat16
VMEM = pltpu.VMEM


def resident(array):
    return pltpu.with_memory_space_constraint(array, VMEM)


def nn(left, right):
    return jnp.dot(left, right, preferred_element_type=f32)


def tn(left, right):
    return lax.dot_general(left, right, (((0,), (0,)), ((), ())), preferred_element_type=f32)


def nt(left, right):
    return lax.dot_general(left, right, (((1,), (1,)), ((), ())), preferred_element_type=f32)


def logistic(v):
    return pl.reciprocal(1.0 + jnp.exp(-v), approx=True)


def by_eight(v):
    return jnp.sum(v.reshape(v.shape[0] // 8, 8, v.shape[1]), axis=0)


def span(base, step, size):
    if isinstance(base, int) and isinstance(step, int):
        return slice(base + step, base + step + size)
    return pl.ds(pl.multiple_of(base + step, 128), size)


def lines(first, size, multiple=8):
    if isinstance(first, int):
        return slice(first, first + size)
    return pl.ds(pl.multiple_of(first, multiple), size)


def doubled(v, axis=0):
    return jnp.concatenate([v, v], axis=axis)


def place_of(shape):
    return lax.broadcasted_iota(jnp.int32, shape, 0)


def across(run, prod, carry, backward):
    place = place_of(run.shape)
    for d in (1, 2, 4):
        seen = place < 8 - d if backward else place >= d
        shift = 8 - d if backward else d
        prod_before = jnp.where(seen, pltpu.roll(prod, shift, 0), 1.0)
        run_before = jnp.where(seen, pltpu.roll(run, shift, 0), 0.0)
        run = run + prod * run_before
        prod = prod * prod_before
    ends = run + prod * carry
    if backward:
        return jnp.where(place < 7, pltpu.roll(ends, 7, 0), carry), ends[0:1, :]
    return jnp.where(place >= 1, pltpu.roll(ends, 1, 0), carry), ends[7:8, :]


def norm_factor(x):
    return lax.rsqrt(jnp.mean(x * x, axis=-1, keepdims=True) + norm_eps)


class Columns(typing.NamedTuple):
    stream: int
    normed: int
    left: int
    grad: int
    outs: int
    sent: int
    wide_a: int
    wide_b: int
    slope: int
    end: int


def columns(width, ff):
    wide = 6 * width + 2 * ff
    return Columns(*(width * i for i in range(7)), 6 * width + ff, wide, wide + ff // 2)


class Plan(typing.NamedTuple):
    hop: int
    chunks: int
    per_row: int
    sections: int


def forward_turn(plan, info):
    c = info[2] - plan.hop * info[0]
    return jnp.clip(c, 0, plan.chunks - 1), (c >= 0) & (c < plan.chunks)


def backward_turn(plan, info):
    j = info[3] - plan.hop * (plan.sections - 1 - info[0])
    return jnp.clip(j, 0, plan.chunks - 1), (j >= 0) & (j < plan.chunks)


def backward_chunk(plan, j):
    behind = lax.rem(j, plan.per_row)
    return j - behind + plan.per_row - 1 - behind


def loop(count, step):
    lax.fori_loop(0, count, lambda i, carry: (step(i), carry)[1], 0)


def unrolled(count, step):
    for b in range(count):
        step(b)


def into_runs(held, start, rows_now, column, width, p_s):
    runs = rows_now // 8

    def step(k):
        cols = span(column, 128 * k, 128)
        p_s[:, 0:128] = held[pl.ds(start, rows_now), cols].astype(f32)
        for m in range(rows_now // 16):
            pair = [p_s[pl.ds(2 * m + h, 8, stride=runs), :] for h in (0, 1)]
            held[pl.ds(pl.multiple_of(start + 16 * m, 16), 16), cols] = jnp.concatenate(pair, axis=0).astype(bf16)

    loop(width // 128, step)


def forward_kernel(
    plan, recv, w1, w2, vec,
    sc_in, held_in, msk_in, hs_in, nh_in, send, sc, held, msk, hs, nh,
    pm, p_2, q_2, e_2, g_2, nx, kp,
):
    rows_now, width = recv.shape
    ff = w1.shape[1]
    hidden = ff // 2
    col = columns(width, ff)
    c, active = forward_turn(plan, sc)
    start = pl.multiple_of(c * rows_now, rows_now)
    rows = pl.ds(start, rows_now)
    mixer = sc[1] == 0
    tail = width + ff
    tiles = rows_now // 16
    narrow = lambda base: slice(base, base + width)

    def at(r, size):
        return pl.ds(pl.multiple_of(start + r, 16), size)

    @pl.when(active & (sc[0] > 0))
    def _():
        held[rows, narrow(col.stream)] = recv[...]

    @pl.when(active & (sc[0] == 0))
    def _():
        into_runs(held, start, rows_now, col.stream, width, pm)

    @pl.when(active & mixer)
    def _():
        gain = vec[:, :width]

        def norm_step(i):
            here = at(tall * i, tall)
            x = held[here, narrow(col.stream)].astype(f32)
            factor = norm_factor(x)
            normed = x * factor * gain
            nx[lines(24 + tall * i, tall, 8), :] = normed
            held[here, narrow(col.normed)] = normed.astype(bf16)
            msk[here, 6:7] = factor
            kp[lines(tall * i, tall, 8), :] = jnp.broadcast_to(msk[here, 0:1], (tall, 128))

        unrolled(rows_now // tall, norm_step)
        place = place_of((8, width))
        for g in range(0, 24, 8):
            rolled = pltpu.roll(nx[rows_now + g : rows_now + g + 8, :], 1, 0)
            nx[g : g + 8, :] = jnp.where(place == 0, nh[g : g + 8, :], rolled)
            nh[g : g + 8, :] = rolled

        def conv_step(i):
            here = at(tall * i, tall)
            conv = nx[lines(24 + tall * i, tall, 8), :] * vec[:, width : 2 * width]
            for j in range(1, ff // width):
                tap = vec[:, (1 + j) * width : (2 + j) * width]
                earlier = nx[lines(24 - 8 * j + tall * i, tall, 8), :]
                conv = conv + earlier * (msk[here, j - 1 : j] * tap)
            held[here, narrow(col.left)] = conv.astype(bf16)

        unrolled(rows_now // tall, conv_step)

        def hidden_step(b):
            own = span(0, lane_block * b, lane_block)
            conv16 = held[rows, narrow(col.left)]
            p_s, q_s, e_s, g_s = (ref.at[b % 2] for ref in (p_2, q_2, e_2, g_2))
            p_s[...] = nn(conv16, w1[:, own])
            e_s[...] = nn(conv16, w1[:, span(hidden, lane_block * b, lane_block)])
            g_s[...] = nt(held[rows, narrow(col.normed)], w2[span(hidden, lane_block * b, lane_block), :])
            bias = vec[:, span(tail, lane_block * b, lane_block)]
            on = lambda base: span(base, lane_block * b, lane_block)
            run = prod = None
            for m in range(tiles):
                r = 16 * m
                update = logistic(p_s[r : r + 16, :] + bias)
                held[at(r, 16), on(col.wide_a)] = update.astype(bf16)
                decay = (1.0 - update) * doubled(kp[r : r + 16, :], 1)
                fresh = update * e_s[r : r + 16, :]
                for h in (0, 8):
                    a, v = decay[h : h + 8, :], fresh[h : h + 8, :]
                    run, prod = (v, a) if run is None else (a * run + v, prod * a)
                    p_s[r + h : r + h + 8, :] = prod
                    q_s[r + h : r + h + 8, :] = run
            inward, last = across(run, prod, hs[0:1, own], False)
            hs[0:1, own] = last
            inward = doubled(inward)
            for m in range(tiles):
                r = 16 * m
                states = q_s[r : r + 16, :] + p_s[r : r + 16, :] * inward
                gate = g_s[r : r + 16, :]
                sig = logistic(gate)
                act = gate * sig
                held[at(r, 16), on(col.wide_b)] = (states * act).astype(bf16)
                held[at(r, 16), on(col.slope)] = act.astype(bf16)
                held[at(r, 16), on(col.wide_b + hidden)] = (states * (sig + act * (1.0 - sig))).astype(bf16)
                update = held[at(r, 16), on(col.wide_a)].astype(f32)
                held[at(r, 16), on(col.wide_a + hidden)] = (update * (e_s[r : r + 16, :] - states)).astype(bf16)

        unrolled(hidden // lane_block, hidden_step)

        def out_step(b):
            own = span(0, lane_block * b, lane_block)
            x = held[rows, span(col.stream, lane_block * b, lane_block)].astype(f32)
            result = (x + nn(held[rows, col.wide_b : col.wide_b + hidden], w2[:hidden, own])).astype(bf16)
            send[:, own] = result
            held[rows, span(col.outs, lane_block * b, lane_block)] = result

        unrolled(width // lane_block, out_step)

    @pl.when(active & jnp.logical_not(mixer))
    def _():
        gain = vec[:, :width]

        def norm_step(i):
            here = at(tall * i, tall)
            x = held[here, narrow(col.stream)].astype(f32)
            factor = norm_factor(x)
            msk[here, 6:7] = factor
            held[here, narrow(col.left)] = (x * factor * gain).astype(bf16)

        unrolled(rows_now // tall, norm_step)

        norm16 = held[rows, narrow(col.left)]
        for lo in range(0, ff, lane_block):
            hi = lo + lane_block
            h = nn(norm16, w1[:, lo:hi]) + vec[:, width + lo : width + hi]
            square = h * h
            bend = jnp.tanh(h * (0.7978845608 + (0.7978845608 * 0.044715) * square))
            half = 0.5 + 0.5 * bend
            held[rows, col.wide_b + lo : col.wide_b + hi] = (h * half).astype(bf16)
            slope = half + (h * (1.0 - bend * bend)) * (
                0.5 * 0.7978845608 + (0.5 * 0.7978845608 * 3.0 * 0.044715) * square
            )
            held[rows, col.wide_a + lo : col.wide_a + hi] = slope.astype(bf16)
        down = nn(held[rows, col.wide_b : col.slope], w2[...])
        held[rows, narrow(col.normed)] = down.astype(bf16)
        x = held[rows, narrow(col.stream)].astype(f32)
        result = (x + (down * vec[:, tail : tail + width] + vec[:, tail + width : tail + 2 * width])).astype(bf16)
        send[...] = result
        held[rows, narrow(col.outs)] = result

    sc[2] = sc[2] + 1


def norm_backward(x, factor, gain, grad_normed, grads_wide, vacc):
    width = x.shape[1]
    scaled = x * factor
    vacc[:, :width] = vacc[:, :width] + by_eight(grad_normed * scaled)
    e = grad_normed * gain
    level = jnp.mean(e * scaled, axis=-1, keepdims=True)
    return (grads_wide + factor * (e - scaled * level)).astype(bf16)


def backward_kernel(
    plan, recv, w1, w2, vec,
    sc_in, held_in, msk_in, vacc_in, wc_in, gh_in, send, sc, held, msk, vacc, wc, gh,
    pm, p_2, q_2, g_2, nx, gx, gn, kp,
):
    rows_now, width = recv.shape
    ff = w1.shape[1]
    hidden = ff // 2
    col = columns(width, ff)
    j, active = backward_turn(plan, sc)
    start = pl.multiple_of(backward_chunk(plan, j) * rows_now, rows_now)
    rows = pl.ds(start, rows_now)
    mixer = sc[1] == 0
    tail = width + ff
    tiles = rows_now // 16
    narrow = lambda base: slice(base, base + width)

    def at(r, size):
        return pl.ds(pl.multiple_of(start + r, 16), size)

    def before(size):
        return pl.ds(pl.multiple_of(jnp.maximum(start - size, 0), 16), size)

    @pl.when(active & (sc[0] < plan.sections - 1))
    def _():
        held[rows, narrow(col.grad)] = recv[...]

    @pl.when(active & (sc[0] == plan.sections - 1))
    def _():
        into_runs(held, start, rows_now, col.grad, width, pm)

    def add(cols, value):
        vacc[:, cols] = vacc[:, cols] + value

    @pl.when(active & mixer)
    def _():
        gain = vec[:, :width]

        def norm_step(i):
            here = at(tall * i, tall)
            nx[lines(24 + tall * i, tall, 8), :] = held[here, narrow(col.normed)].astype(f32)
            kp[lines(tall * i, tall, 8), :] = jnp.broadcast_to(msk[here, 0:1], (tall, 128))

        unrolled(rows_now // tall, norm_step)
        n_before = held[before(32), narrow(col.normed)].astype(f32)[8:32, :]
        place = place_of((8, width))
        for g in range(0, 24, 8):
            nx[g : g + 8, :] = pltpu.roll(
                jnp.where(place == 7, n_before[g : g + 8, :], nx[rows_now + g : rows_now + g + 8, :]), 1, 0
            )

        def hidden_step(b):
            own = span(0, lane_block * b, lane_block)
            on = lambda base: span(base, lane_block * b, lane_block)
            p_s, q_s, g_s = (ref.at[0] for ref in (p_2, q_2, g_2))
            g_s[...] = nt(held[rows, narrow(col.grad)], w2[own, :])
            run = prod = None
            for m in range(tiles - 1, -1, -1):
                r = 16 * m
                grad_merged = g_s[r : r + 16, :]
                turn = held[at(r, 16), on(col.wide_b + hidden)].astype(f32)
                held[at(r, 16), on(col.wide_b + hidden)] = (grad_merged * turn).astype(bf16)
                update = held[at(r, 16), on(col.wide_a)].astype(f32)
                decay = (1.0 - update) * doubled(kp[r : r + 16, :], 1)
                grad_states = grad_merged * held[at(r, 16), on(col.slope)].astype(f32)
                for h in (8, 0):
                    a, v = decay[h : h + 8, :], grad_states[h : h + 8, :]
                    if run is None:
                        prod = jnp.ones_like(v)
                    else:
                        v = v + run
                    q_s[r + h : r + h + 8, :] = v
                    p_s[r + h : r + h + 8, :] = prod
                    run, prod = a * v, prod * a
            inward, last = across(run, prod, wc[0:1, own], True)
            wc[0:1, own] = last
            inward = doubled(inward)
            total = jnp.zeros((8, lane_block), f32)
            for m in range(tiles):
                r = 16 * m
                carried = q_s[r : r + 16, :] + p_s[r : r + 16, :] * inward
                update = held[at(r, 16), on(col.wide_a)].astype(f32)
                up16 = (carried * held[at(r, 16), on(col.wide_a + hidden)].astype(f32)).astype(bf16)
                held[at(r, 16), on(col.wide_a)] = up16
                held[at(r, 16), on(col.wide_a + hidden)] = (carried * update).astype(bf16)
                up = up16.astype(f32)
                total = total + (up[0:8, :] + up[8:16, :])
            add(on(tail), total)

        loop(hidden // lane_block, hidden_step)

        def product_step(b):
            own = span(0, lane_block * b, lane_block)
            gx[0:rows_now, own] = nt(held[rows, col.wide_a : col.wide_b], w1[own, :])
            gn[:, own] = nn(held[rows, col.wide_b + hidden : col.slope], w2[hidden:, own])

        unrolled(width // lane_block, product_step)
        for g in range(0, 24, 8):
            rolled = pltpu.roll(gx[g : g + 8, :], 7, 0)
            gx[rows_now + g : rows_now + g + 8, :] = jnp.where(place == 7, gh[g : g + 8, :], rolled)
            gh[g : g + 8, :] = rolled

        def out_step(i):
            here = at(tall * i, tall)
            x = held[here, narrow(col.stream)].astype(f32)
            factor = msk[here, 6:7]
            base = tall * i
            grad_conv = gx[lines(base, tall, 8), :]
            grad_normed = gn[lines(base, tall, 8), :] + vec[:, width : 2 * width] * grad_conv
            add(slice(width, 2 * width), by_eight(grad_conv * nx[lines(24 + base, tall, 8), :]))
            for k in range(1, ff // width):
                cols = slice((1 + k) * width, (2 + k) * width)
                ahead = gx[lines(base + 8 * k, tall, 8), :]
                grad_normed = grad_normed + ahead * (vec[:, cols] * msk[here, 2 + k : 3 + k])
                earlier = nx[lines(24 - 8 * k + base, tall, 8), :]
                add(cols, by_eight(grad_conv * (earlier * msk[here, k - 1 : k])))
            grads_wide = held[here, narrow(col.grad)].astype(f32)
            result = norm_backward(x, factor, gain, grad_normed, grads_wide, vacc)
            send[lines(base, tall, 16), :] = result
            held[here, narrow(col.sent)] = result

        unrolled(rows_now // tall, out_step)

    @pl.when(active & jnp.logical_not(mixer))
    def _():
        gain = vec[:, :width]

        def scale_step(i):
            here = at(tall * i, tall)
            grads_wide = held[here, narrow(col.grad)].astype(f32)
            down = held[here, narrow(col.normed)].astype(f32)
            add(slice(tail, tail + width), by_eight(grads_wide * down))
            add(slice(tail + width, tail + 2 * width), by_eight(grads_wide))
            held[here, narrow(col.normed)] = (grads_wide * vec[:, tail : tail + width]).astype(bf16)

        unrolled(rows_now // tall, scale_step)

        def hidden_step(b):
            for u in range(1):
                at_b = 1 * lane_block * b + u * lane_block
                on = lambda base: span(base, at_b, lane_block)
                grad_active = nt(held[rows, narrow(col.normed)], w2[on(0), :])
                hid16 = (grad_active * held[rows, on(col.wide_a)].astype(f32)).astype(bf16)
                held[rows, on(col.wide_a)] = hid16
                add(on(width), by_eight(hid16.astype(f32)))

        unrolled(ff // (lane_block * 1), hidden_step)

        def product_step(b):
            own = span(0, lane_block * b, lane_block)
            gn[:, own] = nt(held[rows, col.wide_a : col.wide_b], w1[own, :])

        unrolled(width // lane_block, product_step)

        def out_step(i):
            here = at(tall * i, tall)
            x = held[here, narrow(col.stream)].astype(f32)
            grads_wide = held[here, narrow(col.grad)].astype(f32)
            grad_normed = gn[lines(tall * i, tall, 8), :]
            result = norm_backward(x, msk[here, 6:7], gain, grad_normed, grads_wide, vacc)
            send[lines(tall * i, tall, 16), :] = result
            held[here, narrow(col.sent)] = result

        unrolled(rows_now // tall, out_step)


def weight_kernel(
    plan, rows_now, sc_in, held_in, dw1_in, dw2_in, sc, held, dw1, dw2,
):
    width, ff = dw1.shape
    hidden = ff // 2
    col = columns(width, ff)
    late = sc[0] >= plan.sections // 2
    j = sc[3] - plan.hop * (plan.sections - 1)
    waited = plan.chunks // 2
    first = jnp.where(late, 2 * (j - waited), j)
    count = jnp.where(first < 0, 0, jnp.where(late, 2, 1))

    @pl.when((sc[0] == 0) & (j == -1))
    def _():
        dw1[...] = jnp.zeros_like(dw1)
        dw2[...] = jnp.zeros_like(dw2)

    def unit(i):
        rows = pl.ds(pl.multiple_of(backward_chunk(plan, first + i) * rows_now, rows_now), rows_now)

        def terms(ref, left, right, size, into):
            block = 512
            for lo in range(0, size, block):
                term = tn(left, held[rows, right + lo : right + lo + block])
                cols = slice(into + lo, into + lo + block)
                ref[:, cols] = ref[:, cols] + term

        terms(dw1, held[rows, col.left : col.left + width], col.wide_a, ff, 0)
        upper = jnp.where(sc[1] == 0, col.grad, col.normed)
        terms(dw2, held[rows, span(upper, 0, width)], col.wide_b, hidden, 0)
        terms(dw2, held[rows, col.normed : col.normed + width], col.wide_b + hidden, hidden, hidden)

    loop(count, unit)

    sc[3] = sc[3] + 1


def load_kernel(sections, x_hbm, g_hbm, w1_hbm, w2_hbm, vec_hbm, msk_hbm,
                info, held, w1, w2, vec, msk, hs, nh, wc, gh, vacc, dw1, dw2, blank, sems):
    width, ff = w1.shape
    col = columns(width, ff)
    section = lax.axis_index("section")
    info[0] = section
    info[1] = lax.rem(section, 2)
    info[2] = 0
    info[3] = 0
    moves = [(w1_hbm, w1), (w2_hbm, w2), (vec_hbm, vec), (msk_hbm, msk)]
    copies = [pltpu.make_async_copy(a, b, sems.at[i]) for i, (a, b) in enumerate(moves)]
    first = pltpu.make_async_copy(x_hbm, held.at[:, col.stream : col.stream + width], sems.at[4])
    last = pltpu.make_async_copy(g_hbm, held.at[:, col.grad : col.grad + width], sems.at[5])
    for copy in copies:
        copy.start()

    @pl.when(section == 0)
    def _():
        first.start()

    @pl.when(section == sections - 1)
    def _():
        last.start()

    for ref in (hs, nh, wc, gh, vacc, blank):
        ref[...] = jnp.zeros_like(ref)

    @pl.when(section > 0)
    def _():
        dw1[...] = jnp.zeros_like(dw1)
        dw2[...] = jnp.zeros_like(dw2)

    for copy in copies:
        copy.wait()

    @pl.when(section == 0)
    def _():
        first.wait()

    @pl.when(section == sections - 1)
    def _():
        last.wait()


def piece_of(dw1, dw2, owner, owners):
    width, ff = dw1.shape
    high, broad = width // owners, ff // owners
    count = ff // broad
    low = width // count
    yield 0, high, dw1[pl.ds(pl.multiple_of(high * owner, 8), high), :]
    cols = span(0, broad * owner, broad)
    parts = [dw2[low * q : low * (q + 1), cols] for q in range(count)]
    yield high, low, jnp.concatenate(parts, axis=1)


def finish_kernel(owners, held, dw1, dw2, vacc, outs_out, grads_out, give, keep, sems):
    width, ff = dw1.shape
    col = columns(width, ff)
    copies = [
        pltpu.make_async_copy(held.at[:, base : base + width], target, sems.at[i])
        for i, (base, target) in enumerate(((col.outs, outs_out), (col.sent, grads_out)))
    ]
    for copy in copies:
        copy.start()
    core = lax.rem(lax.axis_index("dp"), 2)
    line = jnp.sum(vacc[...], axis=0, keepdims=True)
    lines = line.shape[1] // 128
    total = jnp.concatenate(
        [line[:, 128 * i : 128 * (i + 1)] for i in range(lines)]
        + [jnp.zeros((give.shape[1] - lines, 128), f32)],
        axis=0,
    )

    def step(z):
        for mine, ref in ((core, keep), (1 - core, give)):
            for at, size, value in piece_of(dw1, dw2, 2 * z + mine, owners):
                ref[z, at : at + size, 0:ff] = value.astype(ref.dtype)
            ref[z, :, ff:] = total.astype(ref.dtype)

    loop(owners // 2, step)
    for copy in copies:
        copy.wait()


def raw_kernel(width, ff, held, outs_out, grads_out, sems):
    col = columns(width, ff)
    copies = [
        pltpu.make_async_copy(held.at[:, base : base + width], target, sems.at[i])
        for i, (base, target) in enumerate(((col.outs, outs_out), (col.sent, grads_out)))
    ]
    for copy in copies:
        copy.start()
    for copy in copies:
        copy.wait()


def share_kernel(chips, keep, got, own, *sends):
    chip = lax.div(lax.axis_index("dp"), 2)
    for ahead, ref in enumerate((own, *sends)):
        z = lax.rem(chip + ahead, chips)
        ref[...] = (keep[z] + got[z].astype(f32)).astype(ref.dtype)


def close_kernel(scale, own, *refs):
    received, (first, second, vectors) = refs[:-3], refs[-3:]
    high = first.shape[0]
    sums = own[...]
    for ref in received:
        sums = sums + ref[...].astype(f32)
    sums = sums * scale
    broad, width = second.shape
    low = sums.shape[0] - high
    ff = first.shape[1]
    first[...] = sums[0:high, 0:ff]
    part = vectors.shape[1]
    count = -(-part // 128)
    lines = sums[0 : 8 * (-(-(len(refs) - 2) * 2 * part // 1024) + 1), ff:]
    lane = lax.broadcasted_iota(jnp.int32, (count, 128), 1)
    chosen = jnp.zeros((count, 128), f32)
    for owner in range(2 * (len(refs) - 2)):
        row, shift = divmod(part * owner, 128)
        turned = pltpu.roll(lines, (128 - shift) % 128, 1)
        mine = jnp.where(lane < 128 - shift, turned[row : row + count], turned[row + 1 : row + 1 + count])
        chosen = jnp.where(lax.axis_index("dp") == owner, mine, chosen)
    vectors[...] = jnp.concatenate([chosen[i : i + 1] for i in range(count)], axis=1)[:, :part]
    for q in range(width // low):
        second[:, low * q : low * (q + 1)] = sums[high:, broad * q : broad * (q + 1)].T


def results_kernel(rows_now, outs_in, grads_in, outs_out, grads_out, pm, fetched, stage, in_sems, out_sems):
    runs = rows_now // 8
    tokens, width = outs_in.shape
    chunks = tokens // rows_now

    for source, target in ((outs_in, outs_out), (grads_in, grads_out)):

        def there(c):
            return pl.ds(pl.multiple_of(c * rows_now, rows_now), rows_now)

        def bring(c, slot):
            return pltpu.make_async_copy(source.at[there(c), :], fetched.at[slot], in_sems.at[slot])

        def send(c, slot):
            return pltpu.make_async_copy(stage.at[slot], target.at[there(c), :], out_sems.at[slot])

        bring(0, 0).start()

        def step(c):
            slot = lax.rem(c, 2)

            @pl.when(c + 1 < chunks)
            def _():
                bring(c + 1, 1 - slot).start()

            @pl.when(c >= 2)
            def _():
                send(c - 2, slot).wait()

            bring(c, slot).wait()
            for k in range(width // 128):
                cols = slice(128 * k, 128 * (k + 1))
                for m in range(rows_now // 16):
                    pair = fetched[slot, 16 * m : 16 * m + 16, cols].astype(f32)
                    for h in (0, 1):
                        pm[k, pl.ds(2 * m + h, 8, stride=runs), :] = pair[8 * h : 8 * h + 8, :]
                stage[slot, :, cols] = pm[k].astype(bf16)
            send(c, slot).start()

        loop(chunks, step)
        for c in range(max(0, chunks - 2), chunks):
            send(c, c % 2).wait()


def forward_scratch(rows, width):
    return (
        [VMEM((rows, 128), f32)]
        + [VMEM((2, rows, lane_block), f32)] * 4
        + [VMEM((rows + 24, width), f32), VMEM((rows, 128), f32)]
    )


def backward_scratch(rows, width):
    return (
        [VMEM((rows, 128), f32)]
        + [VMEM((2, rows, lane_block), f32)] * 3
        + [VMEM((rows + 24, width), f32)] * 2
        + [VMEM((rows, width), f32), VMEM((rows, 128), f32)]
    )


def params():
    return pltpu.CompilerParams(vmem_limit_bytes=vmem_mib * 2**20)


def call(kernel, plain_out, inputs, info, state, scratch, flops, name):
    kept = (pltpu.SMEM(info.shape, info.dtype),) + tuple(VMEM(s.shape, s.dtype) for s in state)
    kept_specs = [pl.BlockSpec(memory_space=pltpu.SMEM)] + [pl.BlockSpec(memory_space=VMEM) for _ in state]
    return pl.pallas_call(
        kernel,
        out_shape=tuple(plain_out) + kept,
        in_specs=[pl.BlockSpec(memory_space=VMEM) for _ in inputs] + kept_specs,
        out_specs=tuple([pl.BlockSpec(memory_space=VMEM) for _ in plain_out] + kept_specs),
        input_output_aliases={len(inputs) + i: len(plain_out) + i for i in range(len(kept))},
        scratch_shapes=scratch,
        compiler_params=params(),
        cost_estimate=pl.CostEstimate(flops=flops, bytes_accessed=0, transcendentals=0),
        name=name,
    )(*inputs, info, *state)


def body(layer_input, resets, first_weights, second_weights, section_vectors, cotangent):
    row_count, seq_length, width = layer_input.shape
    ff = first_weights.shape[2]
    hidden = ff // 2
    vector_width = section_vectors.shape[1]
    section = lax.axis_index("section")
    sections = lax.axis_size("section")
    dp_count = lax.axis_size("dp")
    tokens = row_count * seq_length
    per_row = seq_length // chunk_rows
    chunks = row_count * per_row

    keep = 1.0 - resets.astype(f32)
    keep = jnp.concatenate([jnp.zeros((row_count, 1), f32), keep[:, 1:]], axis=1).reshape(-1)

    def later(v, j):
        return jnp.concatenate([jnp.zeros((j,), f32), v[:-j]])

    def sooner(v, j):
        return jnp.concatenate([v[j:], jnp.zeros((j,), f32)])

    m1 = keep
    m2 = keep * later(keep, 1)
    m3 = m2 * later(keep, 2)
    msk = jnp.stack([m1, m2, m3, sooner(m1, 1), sooner(m2, 2), sooner(m3, 3), m1, m1], axis=1)
    msk = msk.reshape(chunks, 8, chunk_rows // 8, 8).swapaxes(1, 2).reshape(tokens, 8)


    made = (
        pltpu.SMEM((4,), jnp.int32), VMEM((tokens, columns(width, ff).end), bf16),
        VMEM((width, ff), bf16), VMEM((ff, width), bf16), VMEM((1, vector_width), f32), VMEM(msk.shape, f32),
        VMEM((8, hidden), f32), VMEM((24, width), f32), VMEM((8, hidden), f32), VMEM((24, width), f32),
        VMEM((8, vector_width), f32), VMEM((width, ff), f32), VMEM((width, ff), f32),
        VMEM((chunk_rows, width), bf16),
    )
    inputs = [
        layer_input.reshape(tokens, width), cotangent.reshape(tokens, width),
        first_weights[0], second_weights[0], section_vectors, msk,
    ]
    info, held, w1, w2, vec, msk, hs, nh, wc, gh, vacc, dw1, dw2, blank = pl.pallas_call(
        functools.partial(load_kernel, sections),
        out_shape=made,
        in_specs=[pl.BlockSpec(memory_space=pltpu.HBM)] * 6,
        out_specs=(pl.BlockSpec(memory_space=pltpu.SMEM),) + tuple(pl.BlockSpec(memory_space=VMEM) for _ in made[1:]),
        scratch_shapes=[pltpu.SemaphoreType.DMA((6,))],
        compiler_params=params(),
        name="load",
    )(
        *(pltpu.with_memory_space_constraint(v, pltpu.HBM) for v in inputs),
    )
    w1, w2, vec = (resident(v) for v in (w1, w2, vec))

    hop = hop_ticks
    base = per_row - 1 + hop * (sections - 1)
    ticks = base + chunks + hop * (sections - 1)
    plan = Plan(hop, chunks, per_row, sections)
    message = jax.ShapeDtypeStruct((chunk_rows, width), bf16)
    forward_sent, backward_sent = {}, {}
    chunk_flops = 2**10

    for t in range(ticks):
        if t < chunks + hop * (sections - 1):
            sent, info, held, msk, hs, nh = call(
                functools.partial(forward_kernel, plan),
                [message],
                [forward_sent.pop(t - hop, blank), w1, w2, vec],
                info,
                [held, msk, hs, nh],
                forward_scratch(chunk_rows, width),
                chunk_flops,
                "forward_chunk",
            )
            pairs = [(s, s + 1) for s in range(sections - 1) if 0 <= t - hop * s < chunks]
            if pairs:
                forward_sent[t] = lax.ppermute(sent, "section", pairs)
        if t >= base:
            sent, info, held, msk, vacc, wc, gh = call(
                functools.partial(backward_kernel, plan),
                [message],
                [backward_sent.pop(t - hop, blank), w1, w2, vec],
                info,
                [held, msk, vacc, wc, gh],
                backward_scratch(chunk_rows, width),
                chunk_flops,
                "backward_chunk",
            )
            pairs = [
                (s, s - 1) for s in range(1, sections) if 0 <= t - base - hop * (sections - 1 - s) < chunks
            ]
            if pairs:
                backward_sent[t] = lax.ppermute(sent, "section", pairs)
            info, held, dw1, dw2 = call(
                functools.partial(weight_kernel, plan, chunk_rows),
                [],
                [],
                info,
                [held, dw1, dw2],
                [],
                chunk_flops,
                "weight_terms",
            )
    owners = dp_count
    piece = (2 * width // owners, ff + 128)
    vmem_spec, hbm_spec = pl.BlockSpec(memory_space=VMEM), pl.BlockSpec(memory_space=pltpu.HBM)
    flat = jax.ShapeDtypeStruct((tokens, width), bf16)
    scale = (row_count * dp_count * seq_length) ** (-0.5)
    if owners == 8:
        raw_outs, raw_grads, give, own_half = pl.pallas_call(
            functools.partial(finish_kernel, owners),
            out_shape=(
                pltpu.HBM((tokens, width), bf16),
                pltpu.HBM((tokens, width), bf16),
                jax.ShapeDtypeStruct((owners // 2, *piece), bf16),
                VMEM((owners // 2, *piece), f32),
            ),
            in_specs=[vmem_spec] * 4,
            out_specs=(hbm_spec, hbm_spec, vmem_spec, vmem_spec),
            scratch_shapes=[pltpu.SemaphoreType.DMA((2,))],
            compiler_params=params(),
            name="finish",
        )(*(resident(v) for v in (held, dw1, dw2, vacc)))
        got = lax.ppermute(give, "dp", [(d, d ^ 1) for d in range(dp_count)])
        chips = dp_count // 2
        own, *sends = pl.pallas_call(
            functools.partial(share_kernel, chips),
            out_shape=(jax.ShapeDtypeStruct(piece, f32),) + (jax.ShapeDtypeStruct(piece, bf16),) * (chips - 1),
            in_specs=[vmem_spec] * 2,
            out_specs=(vmem_spec,) * chips,
            compiler_params=params(),
            name="share",
        )(resident(own_half), got)
        received = [
            lax.ppermute(sent, "dp", [(d, (d + 2 * ahead) % dp_count) for d in range(dp_count)])
            for ahead, sent in zip(range(1, chips), sends)
        ]
        first, second, vectors = pl.pallas_call(
            functools.partial(close_kernel, scale),
            out_shape=(
                jax.ShapeDtypeStruct((width // owners, ff), f32),
                jax.ShapeDtypeStruct((ff // owners, width), f32),
                jax.ShapeDtypeStruct((1, vector_width // owners), f32),
            ),
            in_specs=[vmem_spec] * chips,
            out_specs=(vmem_spec,) * 3,
            compiler_params=params(),
            name="close",
        )(own, *received)
    else:
        raw_outs, raw_grads = pl.pallas_call(
            functools.partial(raw_kernel, width, ff),
            out_shape=(pltpu.HBM((tokens, width), bf16),) * 2,
            in_specs=[vmem_spec],
            out_specs=(hbm_spec,) * 2,
            scratch_shapes=[pltpu.SemaphoreType.DMA((2,))],
            compiler_params=params(),
            name="raw",
        )(resident(held))
        first = lax.psum_scatter(dw1.astype(bf16), "dp", scatter_dimension=0, tiled=True).astype(f32) * scale
        second = lax.psum_scatter(dw2.astype(bf16), "dp", scatter_dimension=1, tiled=True).astype(f32).T * scale
        vectors = lax.psum_scatter(jnp.sum(vacc, axis=0), "dp", scatter_dimension=0, tiled=True)[None] * scale
    outs, grads = pl.pallas_call(
        functools.partial(results_kernel, chunk_rows),
        out_shape=(flat, flat),
        in_specs=[hbm_spec] * 2,
        out_specs=(hbm_spec,) * 2,
        scratch_shapes=[
            VMEM((width // 128, chunk_rows, 128), f32),
            VMEM((2, chunk_rows, width), bf16),
            VMEM((2, chunk_rows, width), bf16),
            pltpu.SemaphoreType.DMA((2,)),
            pltpu.SemaphoreType.DMA((2,)),
        ],
        compiler_params=params(),
        cost_estimate=pl.CostEstimate(flops=2**33, bytes_accessed=2**23, transcendentals=0),
        name="results",
    )(*(pltpu.with_memory_space_constraint(v, pltpu.HBM) for v in (raw_outs, raw_grads)))
    return (
        outs.reshape(1, row_count, seq_length, width),
        grads.reshape(1, row_count, seq_length, width),
        first[None],
        second[None],
        vectors,
    )


def solution(mesh):
    in_specs = (
        P("dp", None, None),
        P("dp", None),
        P("section", None, None),
        P("section", None, None),
        P("section", None),
        P("dp", None, None),
    )
    out_specs = (
        P("section", "dp", None, None),
        P("section", "dp", None, None),
        P("section", "dp", None),
        P("section", "dp", None),
        P("section", "dp"),
    )
    return jax.shard_map(body, mesh=mesh, in_specs=in_specs, out_specs=out_specs, check_vma=False)
```
